1024 devices in a mesh: batch: 64 (over z, x), proto: 16 (over y, core).
Axes of the slice: x: 4, y: 8, z: 16, core: 2. Of those that a mesh axis runs over, the one named last changes fastest.
Arguments:
- student_feat: bfloat16 [10240, 128], P('batch'), may hold values from -6 to 6
- teacher_feat: bfloat16 [2048, 128], P('batch'), may hold values from -6 to 6
- prototypes: float32 [128, 65536], P(None, 'proto'), may hold values from -0.12 to 0.12
- crop_image: int32 [10240], P('batch'), may hold values from 0 to 1023, as said below
- crop_kind: int32 [10240], P('batch'), may hold values from 0 to 2, as said below
Outputs:
- grad_proto: float32 [128, 65536], P('batch', 'proto')
- grad_student: float32 [10240, 128], P('batch')
The draws below stay inside these ranges and needn't reach their ends.
Inputs may be any that keep to these rules, and one draw needn't show every extreme that they name: `crop_image`: the rows of one device (aligned blocks of 160 rows, block j) name the images j * 16 to (j + 1) * 16 - 1, each exactly 10 times, in an order drawn from the seed. `crop_kind`: each image has exactly one crop of kind 1, one of kind 2 and 8 of kind 0.
All inputs are finite; a program needn't handle non-finite values.
Results may differ from the reference program's by a relative error of at most 0.0033.
Values sent between devices are 32-bit elements; how exact they have to be, the bound alone decides.
No kernel may reach another device: no remote copies, remote signals or barrier semaphores. Data moves between devices by JAX's collectives and lax.ppermute only.
A program may use at most 32 MiB of HBM per device.

```python
import jax
import jax.numpy as jnp
from jax import lax

BOT = 128
PROTOS = 65536
IMG_DEV = 16
CROP_DEV = 160
IMAGES = 1024
CROPS = 10240
TEACHERS = 2048
ITERS = 3
LOSS_SCALE = 16
N_BATCH = 64


def crop_slots(key):
    blocks = CROPS // CROP_DEV
    keys = jax.random.split(key, blocks)
    return jax.vmap(lambda k: jax.random.permutation(k, CROP_DEV))(keys).astype(jnp.int32)


def crop_images(key):
    slots = crop_slots(key)
    blocks = CROPS // CROP_DEV
    base = (jnp.arange(blocks, dtype=jnp.int32) * IMG_DEV)[:, None]
    return (base + slots // 10).reshape(CROPS).astype(jnp.int32)


def cluster_frame(key):
    groups = 32
    frame_key = jax.random.fold_in(key, 101)
    centre_key, rank_key, pick_key = jax.random.split(frame_key, 3)
    centres = jax.random.truncated_normal(centre_key, -4.0, 4.0, (groups, BOT), jnp.float32)
    rank_order = jax.random.permutation(rank_key, groups).astype(jnp.float32)
    weights = -1.2 * jnp.log(rank_order + 1.0)
    image_group = jax.random.categorical(pick_key, weights, shape=(IMAGES,))
    return (centres, image_group)


def draw_crop_image(key, part):
    return crop_images(key)


def draw_crop_kind(key, part):
    slots = crop_slots(key)
    within = slots % 10
    kind = jnp.where(within == 0, 1, jnp.where(within == 1, 2, 0))
    return kind.reshape(CROPS).astype(jnp.int32)


def draw_student_feat(key, part):
    centres, image_group = cluster_frame(key)
    images = crop_images(key)
    key = jax.random.fold_in(key, 5)
    noise_part = jax.random.truncated_normal(key, -4.0, 4.0, (CROPS, BOT), jnp.float32)
    rows = 0.7 * centres[image_group[images]] + noise_part
    return (rows / 1.2207).astype(jnp.bfloat16)


def draw_teacher_feat(key, part):
    centres, image_group = cluster_frame(key)
    key = jax.random.fold_in(key, 7)
    row_group = jnp.repeat(image_group, 2)
    noise_part = jax.random.truncated_normal(key, -4.0, 4.0, (TEACHERS, BOT), jnp.float32)
    rows = 0.7 * centres[row_group] + noise_part
    return (rows / 1.2207).astype(jnp.bfloat16)


def draw_prototypes(key, part):
    centres = cluster_frame(key)[0]
    key = jax.random.fold_in(key, 9)
    mask_key, group_key, lift_key, noise_key = jax.random.split(key, 4)
    aligned = jax.random.bernoulli(mask_key, 0.5, (PROTOS,)).astype(jnp.float32)
    column_group = jax.random.randint(group_key, (PROTOS,), 0, 32)
    lift_scale = jax.random.uniform(lift_key, (PROTOS,), jnp.float32, 0.3, 0.8)
    noise_part = jax.random.truncated_normal(noise_key, -4.0, 4.0, (BOT, PROTOS), jnp.float32)
    aligned_part = centres[column_group].T * (aligned * lift_scale)[None, :]
    return ((noise_part + aligned_part) / 64.0).astype(jnp.float32)


def setup_inputs(seed: int = 0) -> dict:
    streams_of = jax.random.split(jax.random.key(seed), 6)
    return {
        "student_feat": draw_student_feat(jax.random.fold_in(streams_of[5], 71), 0),
        "teacher_feat": draw_teacher_feat(jax.random.fold_in(streams_of[5], 71), 0),
        "prototypes": draw_prototypes(jax.random.fold_in(streams_of[5], 71), 0),
        "crop_image": draw_crop_image(jax.random.fold_in(streams_of[5], 71), 0),
        "crop_kind": draw_crop_kind(jax.random.fold_in(streams_of[5], 71), 0),
    }


EPS = 1e-06
TEACH_TEMP = 0.04
STUD_TEMP = 0.1

def row_unit(x):
    norm = jnp.sqrt(lax.optimization_barrier(jnp.sum(x * x, axis=-1, keepdims=True)) + EPS)
    return (x / norm, norm)

def reference(student_feat, teacher_feat, prototypes, crop_image, crop_kind):
    vnorm = jnp.sqrt(lax.optimization_barrier(jnp.sum(prototypes * prototypes, axis=0)) + EPS)
    unit = prototypes / vnorm[None, :]
    unit_half = unit.astype(jnp.bfloat16)
    t_unit = row_unit(teacher_feat.astype(jnp.float32))[0]
    t_half = t_unit.astype(jnp.bfloat16)
    expo = jnp.exp(jnp.dot(t_half, unit_half, preferred_element_type=jnp.float32) / TEACH_TEMP)
    scale_a = jnp.ones((TEACHERS,), jnp.float32)
    scale_b = jnp.ones((PROTOS,), jnp.float32)
    for step in range(ITERS):
        scale_b = 1.0 / lax.optimization_barrier(jnp.sum(scale_a[:, None] * expo, axis=0))
        scale_a = 1.0 / lax.optimization_barrier(jnp.sum(expo * scale_b[None, :], axis=1))
    target_q = scale_a[:, None] * expo * scale_b[None, :]
    feats = student_feat.reshape(N_BATCH, CROP_DEV, BOT)
    images = crop_image.reshape(N_BATCH, CROP_DEV)
    kinds = crop_kind.reshape(N_BATCH, CROP_DEV)

    def block(carry, items):
        feat, image, kind = items
        s_unit, s_norm = row_unit(feat.astype(jnp.float32))
        s_half = s_unit.astype(jnp.bfloat16)
        logits = jnp.dot(s_half, unit_half, preferred_element_type=jnp.float32)
        s_exp = jnp.exp(logits / STUD_TEMP)
        s_total = lax.optimization_barrier(jnp.sum(s_exp, axis=1))
        prob = s_exp / s_total[:, None]
        first = jnp.take(target_q, 2 * image, axis=0)
        second = jnp.take(target_q, 2 * image + 1, axis=0)
        kcol = kind[:, None]
        target = jnp.where(kcol == 0, 0.5 * first + 0.5 * second, jnp.where(kcol == 1, second, first))
        dlogit = (LOSS_SCALE / STUD_TEMP * (prob - target)).astype(jnp.bfloat16)
        dz = lax.dot_general(dlogit, unit_half, (((1,), (1,)), ((), ())), preferred_element_type=jnp.float32)
        grad_rows = (dz - s_unit * lax.optimization_barrier(jnp.sum(s_unit * dz, axis=1, keepdims=True))) / s_norm
        carry = carry + lax.dot_general(s_half, dlogit, (((0,), (0,)), ((), ())), preferred_element_type=jnp.float32)
        return (carry, grad_rows)
    dunit, grads = lax.scan(block, jnp.zeros((BOT, PROTOS), jnp.float32), (feats, images, kinds))
    dots = lax.optimization_barrier(jnp.sum(unit_half.astype(jnp.float32) * dunit, axis=0))
    grad_proto = (dunit - unit * dots[None, :]) / vnorm[None, :]
    return (grad_proto, grads.reshape(CROPS, BOT))
```

```python
import functools

import jax
import jax.numpy as jnp
from jax import lax
from jax.experimental import pallas as pl
from jax.experimental.pallas import tpu as pltpu
from jax.sharding import Mesh
from jax.sharding import PartitionSpec as P

LOSS_SCALE = 16
EPS = 1e-06
TEACH_GAIN = 25.0
STUD_GAIN = 10.0
GRAD_GAIN = 160.0
BOT = 128
CB = 512
RC = 256
IMGS = 16
F32 = jnp.float32
BF16 = jnp.bfloat16
HI = lax.Precision.HIGHEST
VMEM_LIMIT = 56 * 1024 * 1024
INTERPRET = False


def mm(a, b, ca, cb, precision=None):
    return lax.dot_general(a, b, (((ca,), (cb,)), ((), ())), precision=precision, preferred_element_type=F32)


def call(kernel, out_shape, *args, scratch=(), flops=0):
    specs = pl.BlockSpec(memory_space=pltpu.VMEM)
    return pl.pallas_call(
        kernel,
        out_shape=out_shape,
        in_specs=[specs] * len(args),
        out_specs=jax.tree.map(lambda _: specs, out_shape),
        scratch_shapes=list(scratch),
        compiler_params=pltpu.CompilerParams(vmem_limit_bytes=VMEM_LIMIT),
        cost_estimate=pl.CostEstimate(flops=flops, bytes_accessed=0, transcendentals=0),
        interpret=INTERPRET,
    )(*args)


def row_unit(x):
    norm = jnp.sqrt(jnp.sum(x * x, axis=-1, keepdims=True) + EPS)
    return x / norm, norm


def selector(image, kind, teach_rows):
    shape = (teach_rows, image.shape[1])
    teach = lax.broadcasted_iota(jnp.int32, shape, 0)
    local = jnp.bitwise_and(jnp.broadcast_to(image, shape), IMGS - 1)
    kinds = jnp.broadcast_to(kind, shape)
    weight = jnp.where(kinds == 0, 0.5, jnp.where(jnp.bitwise_and(teach, 1) == 2 - kinds, 1.0, 0.0))
    return jnp.where(local == jnp.right_shift(teach, 1), weight, 0.0)


def spread(rows):
    parts = [jnp.broadcast_to(rows[i : i + 1, :], (128, 128)).T for i in range(rows.shape[0])]
    return jnp.concatenate(parts, axis=0)


def lane_sums(ref, n):
    parts = [jnp.sum(ref[i * 128 : (i + 1) * 128, :].T, axis=0, keepdims=True) for i in range(n)]
    return jnp.concatenate(parts, axis=0)


def peer_sum(ref, peers, size, start, rows):
    total = ref[start : start + rows, :]
    for p in range(1, peers):
        total = total + ref[p * size + start : p * size + start + rows, :]
    return total


def prep_kernel(student, teacher, image, kind, zp, sp):
    s_unit = row_unit(student[...].astype(F32))[0]
    t_unit = row_unit(teacher[...].astype(F32))[0]
    weights = selector(image[...], kind[...], teacher.shape[0])
    mixed = mm(weights.astype(BF16), s_unit.astype(BF16), 1, 0)
    core = lax.axis_index("c")
    th, sh = teacher.shape[0] // 2, student.shape[0] // 2
    first = core == 0
    zp[0:th, :] = jnp.where(first, t_unit[:th], t_unit[th:])
    zp[th : 2 * th, :] = jnp.where(first, mixed[:th], mixed[th:])
    sp[...] = jnp.where(first, s_unit[:sh], s_unit[sh:])


def unit_kernel(own, nx, proto, half, norm, mine):
    start = (lax.axis_index("z") * nx + lax.axis_index("x")) * own

    def step(j, carry):
        cols = pl.ds(pl.multiple_of(j * CB, CB), CB)
        v = proto[:, cols]
        n = jnp.sqrt(jnp.sum(v * v, axis=0, keepdims=True) + EPS)
        unit = v / n
        half[:, cols] = unit.astype(BF16)
        norm[:, cols] = n
        row = lax.broadcasted_iota(jnp.int32, unit.shape, 0)
        mine[:, cols] = jnp.concatenate(
            [jnp.sum(jnp.where(row == start + i, unit, 0.0), axis=0, keepdims=True) for i in range(own)], axis=0
        )
        return carry

    lax.fori_loop(0, proto.shape[1] // CB, step, 0)


def expo_block(t2, uh, gain, scr):
    u2 = jnp.concatenate([uh, uh], axis=0)
    col = jnp.zeros((8, uh.shape[1]), F32)
    for r in range(t2.shape[0] // RC):
        x = mm(t2[r * RC : (r + 1) * RC, :], u2, 1, 0)
        if gain is not None:
            g = gain[r * RC : (r + 1) * RC, :]
            x = x + jnp.concatenate([g] * (uh.shape[1] // 128), axis=1)
        e = jnp.exp(x)
        scr[r * RC : (r + 1) * RC, :] = e
        col = col + jnp.sum(e.reshape(RC // 8, 8, uh.shape[1]), axis=0)
    return jnp.sum(col, axis=0, keepdims=True)


def add_rows(scr, b, acc):
    for r in range(scr.shape[0] // RC):
        rows = slice(r * RC, (r + 1) * RC)
        e = scr[rows, :]
        total = acc[rows, :]
        for k in range(e.shape[1] // 128):
            lanes = slice(k * 128, (k + 1) * 128)
            total = total + e[:, lanes] * b[:, lanes]
        acc[rows, :] = total


def pass1_kernel(nz, groups, th, sh, g_ref, uh_ref, t2, s_half, mixed, pay, scr, acc, es_scr, s_acc):
    size = nz * 2 * th + sh
    for g in range(groups):
        for z in range(nz):
            src = g * size + z * 2 * th
            dst = (g * nz + z) * th
            t = g_ref[src : src + th, :].astype(BF16).astype(F32) * TEACH_GAIN
            hi = t.astype(BF16)
            t2[dst : dst + th, 0:BOT] = hi
            t2[dst : dst + th, BOT : 2 * BOT] = (t - hi.astype(F32)).astype(BF16)
            mixed[dst : dst + th, :] = g_ref[src + th : src + 2 * th, :]
        src = g * size + nz * 2 * th
        s_half[g * sh : (g + 1) * sh, :] = g_ref[src : src + sh, :].astype(BF16)
    acc[...] = jnp.zeros_like(acc)
    s_acc[...] = jnp.zeros_like(s_acc)
    n_t, n_s = t2.shape[0] // 128, s_half.shape[0] // 128
    top = n_t + (n_s + 7) // 8 * 8
    own = pl.multiple_of(lax.axis_index("x") * 2 * sh, 2 * sh)

    def step(j, e1):
        uh = uh_ref[:, pl.ds(pl.multiple_of(j * CB, CB), CB)]
        b = 1.0 / expo_block(t2, uh, None, scr)
        add_rows(scr, b, acc)
        for r in range(s_half.shape[0] // 128):
            rows = slice(r * 128, (r + 1) * 128)
            es = jnp.exp(mm(s_half[rows, :], uh, 1, 0) * STUD_GAIN)
            es_scr[rows, :] = es
            s_acc[rows, :] += sum(es[:, k * 128 : (k + 1) * 128] for k in range(CB // 128))
        return e1 + mm(es_scr[pl.ds(own, 2 * sh), :].astype(BF16), uh, 1, 1)

    e1 = lax.fori_loop(0, uh_ref.shape[1] // CB, step, jnp.zeros((2 * sh, BOT), F32))
    pay[0:n_t, :] = lane_sums(acc, n_t)
    pay[n_t:top, :] = jnp.zeros((top - n_t, 128), F32)
    pay[n_t : n_t + n_s, :] = lane_sums(s_acc, n_s)
    pay[top : top + 2 * sh, :] = e1


def student_kernel(nz, nx, own, peers, n_t, n_s, size, ag1, s_half, uh_ref, out, scale, a_scr):
    scale[...] = spread(GRAD_GAIN / peer_sum(ag1, peers, size, n_t, n_s))
    per = own + 1
    shape = (nz * per, BOT)
    row = lax.broadcasted_iota(jnp.int32, shape, 0)
    lane = lax.broadcasted_iota(jnp.int32, shape, 1)
    base = lax.axis_index("x") * own
    pick = jnp.zeros(shape, jnp.bool_)
    for z in range(nz):
        for i in range(own):
            pick = pick | ((row == z * per + i) & (lane == z * nx * own + base + i))
    picked = jnp.where(pick, 1.0, 0.0).astype(BF16)
    a_scr[...] = mm(picked, s_half[...], 1, 1).astype(BF16)
    n_c = uh_ref.shape[1] // 128

    def step(j, carry):
        uh = uh_ref[:, pl.ds(pl.multiple_of(j * CB, CB), CB)]
        d = jnp.zeros((nz * per, CB), F32)
        dots = jnp.zeros((8, CB), F32)
        for r in range(s_half.shape[0] // 128):
            rows = slice(r * 128, (r + 1) * 128)
            logits = mm(s_half[rows, :], uh, 1, 0)
            f = scale[rows, :]
            prob = jnp.exp(logits * STUD_GAIN) * jnp.concatenate([f] * (CB // 128), axis=1)
            dots = dots + jnp.sum((prob * logits).reshape(16, 8, CB), axis=0)
            d = d + mm(a_scr[:, rows], prob.astype(BF16), 1, 0)
        dot_row = jnp.sum(dots, axis=0, keepdims=True)
        for k in range(CB // 128):
            lanes = slice(k * 128, (k + 1) * 128)
            for z in range(nz):
                for i in range(own):
                    out[z, pl.ds(i * n_c + j * (CB // 128) + k, 1), :] = d[z * per + i : z * per + i + 1, lanes]
                out[z, pl.ds(own * n_c + j * (CB // 128) + k, 1), :] = dot_row[:, lanes]
        return carry

    lax.fori_loop(0, uh_ref.shape[1] // CB, step, 0)


def pass2_kernel(peers, size, n_t, ag, t2, uh_ref, pay, log_a, scr, acc, gain):
    la = -jnp.log(peer_sum(ag, peers, size, 0, n_t))
    log_a[...] = la
    gain[...] = spread(la)
    acc[...] = jnp.zeros_like(acc)

    def step(j, carry):
        uh = uh_ref[:, pl.ds(pl.multiple_of(j * CB, CB), CB)]
        b = 1.0 / expo_block(t2, uh, gain, scr)
        add_rows(scr, b, acc)
        return carry

    lax.fori_loop(0, uh_ref.shape[1] // CB, step, 0)
    pay[...] = lane_sums(acc, n_t)


def pass3_kernel(nz, th, peers, size, n_t, ag, log_a1, t2, uh_ref, pay, log_a2, b_out, scr, acc, gain):
    la = log_a1[...] - jnp.log(peer_sum(ag, peers, size, 0, n_t))
    log_a2[...] = la
    gain[...] = spread(la)
    acc[...] = jnp.zeros_like(acc)
    z, x = lax.axis_index("z"), lax.axis_index("x")
    starts = [pl.multiple_of(((2 * x + c) * nz + z) * th, th) for c in range(2)]

    def step(j, t_sum):
        cols = pl.ds(pl.multiple_of(j * CB, CB), CB)
        uh = uh_ref[:, cols]
        b = 1.0 / expo_block(t2, uh, gain, scr)
        b_out[:, cols] = b
        add_rows(scr, b, acc)
        mine = jnp.concatenate([scr[pl.ds(s, th), :] for s in starts], axis=0) * b
        return t_sum + mm(mine.astype(BF16), uh, 1, 1)

    t_sum = lax.fori_loop(0, uh_ref.shape[1] // CB, step, jnp.zeros((2 * th, BOT), F32))
    pay[0:n_t, :] = lane_sums(acc, n_t)
    pay[n_t:, :] = t_sum


def final_kernel(
    nz, nx, own, th, sh, peers, size1, n_s, size3, n_t,
    ag3, log_a2, b_ref, t2, uh_ref, mixed, d1, ag1, student, image, kind, norm, mine,
    gp, gs, gain, ma, s_scr, d_scr,
):
    x, z = lax.axis_index("x"), lax.axis_index("z")
    ratio = 1.0 / peer_sum(ag3, peers, size3, 0, n_t)
    gain[...] = spread(ratio)
    s_scr[...] = spread(1.0 / peer_sum(ag1, peers, size1, n_t, n_s))
    starts = [pl.multiple_of(((2 * x + c) * nz + z) * th, th) for c in range(2)]
    own_ratio = jnp.concatenate([gain[pl.ds(s, th), :] for s in starts], axis=0)
    t_sum = peer_sum(ag3, peers, size3, n_t, 2 * th) * own_ratio
    top = n_t + (n_s + 7) // 8 * 8
    e1 = peer_sum(ag1, peers, size1, top, 2 * sh) * s_scr[pl.ds(pl.multiple_of(x * 2 * sh, 2 * sh), 2 * sh), :]
    weights = selector(image[...], kind[...], 2 * th)
    dz = GRAD_GAIN * (e1 - mm(weights, t_sum, 0, 0, HI))
    s_unit, s_norm = row_unit(student[...].astype(F32))
    gs[...] = (dz - s_unit * jnp.sum(s_unit * dz, axis=1, keepdims=True)) / s_norm
    gain[...] = spread(jnp.exp(log_a2[...]) * ratio)
    for i in range(n_t):
        rows = slice(i * 128, (i + 1) * 128)
        ma[:, rows] = (mixed[rows, :] * gain[rows, :]).T.astype(BF16)
    total = d1[0]
    for k in range(1, nz):
        total = total + d1[k]
    d_scr[...] = total
    n_c = uh_ref.shape[1] // 128
    start = (z * nx + x) * own

    def step(j, carry):
        cols = pl.ds(pl.multiple_of(j * CB, CB), CB)
        uh = uh_ref[:, cols]
        u2 = jnp.concatenate([uh, uh], axis=0)
        d2 = jnp.zeros((BOT, CB), F32)
        for r in range(t2.shape[0] // RC):
            rows = slice(r * RC, (r + 1) * RC)
            e = jnp.exp(mm(t2[rows, :], u2, 1, 0)).astype(BF16)
            d2 = d2 + mm(ma[:, rows], e, 1, 0)
        d2 = d2 * (b_ref[:, cols] * GRAD_GAIN)
        dots2 = jnp.sum(uh.astype(F32) * d2, axis=0, keepdims=True)
        row = lax.broadcasted_iota(jnp.int32, d2.shape, 0)

        def early(i):
            return jnp.concatenate(
                [d_scr[pl.ds(i * n_c + j * (CB // 128) + k, 1), :] for k in range(CB // 128)], axis=1
            )

        dots = early(own) - dots2
        n = norm[:, cols]
        outs = []
        for i in range(own):
            late = jnp.sum(jnp.where(row == start + i, d2, 0.0), axis=0, keepdims=True)
            outs.append((early(i) - late - mine[i : i + 1, cols] * dots) / n)
        gp[:, cols] = jnp.concatenate(outs, axis=0)
        return carry

    lax.fori_loop(0, uh_ref.shape[1] // CB, step, 0)


def sds(shape, dtype=F32):
    return jax.ShapeDtypeStruct(shape, dtype)


def per_device(sizes, student_feat, teacher_feat, prototypes, crop_image, crop_kind):
    nz, nx, ny, nc = sizes
    peers = ny * nc
    groups = nx * nc
    crops, teach = student_feat.shape[0], teacher_feat.shape[0]
    th, sh = teach // 2, crops // 2
    cols = prototypes.shape[1]
    own = BOT // (nz * nx)
    teachers, gathered = teach * nz * nx, crops * nx
    n_t, n_s = teachers // 128, gathered // 128
    image, kind = crop_image.reshape(1, crops), crop_kind.reshape(1, crops)
    fl = 2 * teachers * cols * 256

    zp, sp = call(prep_kernel, (sds((2 * th, BOT)), sds((sh, BOT))), student_feat, teacher_feat, image, kind)
    got = lax.all_to_all(jnp.broadcast_to(zp[None], (nz, 2 * th, BOT)), "z", 0, 0, tiled=True)
    half, norm, mine = call(
        functools.partial(unit_kernel, own, nx), (sds((BOT, cols), BF16), sds((1, cols)), sds((own, cols))), prototypes
    )
    pack = jnp.concatenate([got.reshape(nz * 2 * th, BOT), sp], axis=0)
    everything = lax.all_gather(pack, ("x", "c"), tiled=True)

    big = [pltpu.VMEM((teachers, CB), F32), pltpu.VMEM((teachers, 128), F32)]
    size1 = n_t + (n_s + 7) // 8 * 8 + crops
    t2, s_half, mixed, pay1 = call(
        functools.partial(pass1_kernel, nz, groups, th, sh),
        (sds((teachers, 256), BF16), sds((gathered, BOT), BF16), sds((teachers, BOT)), sds((size1, 128))),
        everything,
        half,
        scratch=big + [pltpu.VMEM((gathered, CB), F32), pltpu.VMEM((gathered, 128), F32)],
        flops=fl,
    )
    ag1 = lax.all_gather(pay1, ("y", "c"), tiled=True)
    d1 = call(
        functools.partial(student_kernel, nz, nx, own, peers, n_t, n_s, size1),
        sds((nz, (own + 1) * cols // 128, 128)),
        ag1,
        s_half,
        half,
        scratch=[pltpu.VMEM((gathered, 128), F32), pltpu.VMEM((nz * (own + 1), gathered), BF16)],
        flops=fl // 4,
    )
    d1 = lax.all_to_all(d1, "z", 0, 0, tiled=True)
    pay2, log_a1 = call(
        functools.partial(pass2_kernel, peers, size1, n_t),
        (sds((n_t, 128)), sds((n_t, 128))),
        ag1,
        t2,
        half,
        scratch=big + [pltpu.VMEM((teachers, 128), F32)],
        flops=fl,
    )
    ag2 = lax.all_to_all(jnp.broadcast_to(pay2[None], (peers, n_t, 128)), ("y", "c"), 0, 0, tiled=True)
    pay3, log_a2, b3 = call(
        functools.partial(pass3_kernel, nz, th, peers, n_t, n_t),
        (sds((n_t + teach, 128)), sds((n_t, 128)), sds((1, cols))),
        ag2.reshape(peers * n_t, 128),
        log_a1,
        t2,
        half,
        scratch=big + [pltpu.VMEM((teachers, 128), F32)],
        flops=fl,
    )
    ag3 = lax.all_gather(pay3, ("y", "c"), tiled=True)
    grad_proto, grad_student = call(
        functools.partial(final_kernel, nz, nx, own, th, sh, peers, size1, n_s, n_t + teach, n_t),
        (sds((own, cols)), sds((crops, BOT))),
        ag3, log_a2, b3, t2, half, mixed, d1, ag1, student_feat, image, kind, norm, mine,
        scratch=[
            pltpu.VMEM((teachers, 128), F32),
            pltpu.VMEM((BOT, teachers), BF16),
            pltpu.VMEM((gathered, 128), F32),
            pltpu.VMEM(((own + 1) * cols // 128, 128), F32),
        ],
        flops=fl * 2,
    )
    return grad_proto, grad_student


def build(devices):
    grid = Mesh(devices, ("z", "x", "y", "c"))
    batch, proto = ("z", "x"), ("y", "c")
    return jax.shard_map(
        functools.partial(per_device, devices.shape),
        mesh=grid,
        in_specs=(P(batch, None), P(batch, None), P(None, proto), P(batch), P(batch)),
        out_specs=(P(batch, proto), P(batch, None)),
        check_vma=False,
    )


def solution(mesh):
    return build(mesh.devices.reshape(16, 4, 8, 2))
```

```python
import functools

import jax
import jax.numpy as jnp
from jax import lax
from jax.experimental import pallas as pl
from jax.experimental.pallas import tpu as pltpu
from jax.sharding import Mesh
from jax.sharding import PartitionSpec as P

LOSS_SCALE = 16
EPS = 1e-06
LOG2E = 1.4426950408889634
TEACH_GAIN = 25.0 * LOG2E
STUD_GAIN = 10.0 * LOG2E
GRAD_GAIN = 160.0
BOT = 128
CB = 512
RC = 256
IMGS = 16
F32 = jnp.float32
BF16 = jnp.bfloat16
HI = lax.Precision.HIGHEST
VMEM_LIMIT = 28 * 1024 * 1024
INTERPRET = False


def mm(a, b, ca, cb, precision=None):
    return lax.dot_general(a, b, (((ca,), (cb,)), ((), ())), precision=precision, preferred_element_type=F32)


def call(kernel, out_shape, *args, scratch=(), flops=0, limit=VMEM_LIMIT):
    specs = pl.BlockSpec(memory_space=pltpu.VMEM)
    return pl.pallas_call(
        kernel,
        out_shape=out_shape,
        in_specs=[specs] * len(args),
        out_specs=jax.tree.map(lambda _: specs, out_shape),
        scratch_shapes=list(scratch),
        compiler_params=pltpu.CompilerParams(vmem_limit_bytes=limit),
        cost_estimate=pl.CostEstimate(flops=flops, bytes_accessed=0, transcendentals=0),
        interpret=INTERPRET,
    )(*args)


def row_unit(x):
    norm = jnp.sqrt(jnp.sum(x * x, axis=-1, keepdims=True) + EPS)
    return x / norm, norm


def selector(image, kind, teach_rows):
    shape = (teach_rows, image.shape[1])
    teach = lax.broadcasted_iota(jnp.int32, shape, 0)
    local = jnp.bitwise_and(jnp.broadcast_to(image, shape), IMGS - 1)
    kinds = jnp.broadcast_to(kind, shape)
    weight = jnp.where(kinds == 0, 0.5, jnp.where(jnp.bitwise_and(teach, 1) == 2 - kinds, 1.0, 0.0))
    return jnp.where(local == jnp.right_shift(teach, 1), weight, 0.0)


def spread(rows):
    parts = [jnp.broadcast_to(rows[i : i + 1, :], (128, 128)).T for i in range(rows.shape[0])]
    return jnp.concatenate(parts, axis=0)


def lane_sums(ref, n):
    parts = [jnp.sum(ref[i * 128 : (i + 1) * 128, :].T, axis=0, keepdims=True) for i in range(n)]
    return jnp.concatenate(parts, axis=0)


def prep_kernel(nz, student, teacher, image, kind, zp, sp):
    s_unit = row_unit(student[...].astype(F32))[0]
    t_unit = row_unit(teacher[...].astype(F32))[0]
    weights = selector(image[...], kind[...], teacher.shape[0])
    mixed = mm(weights.astype(BF16), s_unit.astype(BF16), 1, 0)
    th, sh = teacher.shape[0] // 2, student.shape[0] // 2
    first = lax.axis_index("c") == 0
    t = jnp.where(first, t_unit[:th], t_unit[th:])
    m = jnp.where(first, mixed[:th], mixed[th:])
    for p in range(nz):
        zp[p, 0:th, :] = t
        zp[p, th : 2 * th, :] = m
    sp[...] = jnp.where(first, s_unit[:sh], s_unit[sh:])


def unit_kernel(own, nx, proto, half, norm, mine):
    start = (lax.axis_index("z") * nx + lax.axis_index("x")) * own

    def step(j, carry):
        cols = pl.ds(pl.multiple_of(j * CB, CB), CB)
        v = proto[:, cols]
        n = jnp.sqrt(jnp.sum(v * v, axis=0, keepdims=True) + EPS)
        unit = v / n
        half[:, cols] = unit.astype(BF16)
        norm[:, cols] = n
        row = lax.broadcasted_iota(jnp.int32, unit.shape, 0)
        mine[:, cols] = jnp.concatenate(
            [jnp.sum(jnp.where(row == start + i, unit, 0.0), axis=0, keepdims=True) for i in range(own)], axis=0
        )
        return carry

    lax.fori_loop(0, proto.shape[1] // CB, step, 0)


def pack_kernel(nz, nx, got, sp, near, late):
    th = got.shape[1] // 2
    for p in range(nx):
        for z in range(nz):
            near[p, z * th : (z + 1) * th, :] = got[z, 0:th, :]
            late[p, z * th : (z + 1) * th, :] = got[z, th : 2 * th, :]
        near[p, nz * th :, :] = sp[...]


def powers(t2, u2, gain, r):
    x = mm(t2[r * RC : (r + 1) * RC, :], u2, 1, 0)
    if gain is not None:
        x = x + jnp.concatenate([gain[r * RC : (r + 1) * RC, :]] * (CB // 128), axis=1)
    return jnp.exp2(x)


def balance(t2, uh_ref, gain, scr, acc, first, finish, carry):
    n = uh_ref.shape[1] // CB
    acc[...] = jnp.zeros_like(acc)

    def block(j):
        return uh_ref[:, pl.ds(pl.multiple_of(j * CB, CB), CB)]

    def half(j, src, dst, b, carry):
        col = jnp.zeros((8, CB), F32)
        if dst is not None:
            uh = block(j)
            u2 = jnp.concatenate([uh, uh], axis=0)
        for r in range(t2.shape[0] // RC):
            rows = slice(r * RC, (r + 1) * RC)
            if dst is not None:
                e = powers(t2, u2, gain, r)
                scr[dst, rows, :] = e
                col = col + jnp.sum(e.reshape(RC // 8, 8, CB), axis=0)
            if src is not None:
                e = scr[src, rows, :]
                total = acc[rows, :]
                for k in range(CB // 128):
                    lanes = slice(k * 128, (k + 1) * 128)
                    total = total + e[:, lanes] * b[:, lanes]
                acc[rows, :] = total
        if src is not None and finish is not None:
            carry = finish(j - 1, b, scr.at[src], block(j - 1), carry)
        if dst is not None and first is not None:
            carry = first(uh, carry)
        return 1.0 / jnp.sum(col, axis=0, keepdims=True), carry

    b, carry = half(0, None, 0, None, carry)

    def step(i, state):
        b, carry = half(2 * i + 1, 0, 1, *state)
        return half(2 * i + 2, 1, 0, b, carry)

    b, carry = lax.fori_loop(0, n // 2 - 1, step, (b, carry))
    b, carry = half(n - 1, 0, 1, b, carry)
    return half(n, 1, None, b, carry)[1]


def pass1_kernel(nz, nx, peers, th, sh, near, other, uh_ref, t2, s_half, pay, scr, acc, es_scr, s_acc):
    rows_t = nz * th
    core = lax.axis_index("c")
    for g in range(2 * nx):
        both = jnp.where(core == g % 2, near[g // 2], other[g // 2])
        t = both[:rows_t].astype(BF16).astype(F32) * TEACH_GAIN
        hi = t.astype(BF16)
        t2[g * rows_t : (g + 1) * rows_t, 0:BOT] = hi
        t2[g * rows_t : (g + 1) * rows_t, BOT : 2 * BOT] = (t - hi.astype(F32)).astype(BF16)
        s_half[g * sh : (g + 1) * sh, :] = both[rows_t:].astype(BF16)
    s_acc[...] = jnp.zeros_like(s_acc)
    n_t, n_s = t2.shape[0] // 128, s_half.shape[0] // 128
    own = pl.multiple_of(lax.axis_index("x") * 2 * sh, 2 * sh)

    def first(uh, e1):
        for r in range(s_half.shape[0] // 128):
            rows = slice(r * 128, (r + 1) * 128)
            es = jnp.exp2(mm(s_half[rows, :], uh, 1, 0) * STUD_GAIN)
            es_scr[rows, :] = es
            s_acc[rows, :] += sum(es[:, k * 128 : (k + 1) * 128] for k in range(CB // 128))
        return e1 + mm(es_scr[pl.ds(own, 2 * sh), :].astype(BF16), uh, 1, 1)

    e1 = balance(t2, uh_ref, None, scr, acc, first, None, jnp.zeros((2 * sh, BOT), F32))
    sums = lane_sums(acc, n_t)
    totals = lane_sums(s_acc, n_s)
    part = 2 * sh // peers
    fill = jnp.zeros((16 - part - n_s, BOT), F32)
    for p in range(peers):
        pay[p, 0:n_t, :] = sums
        pay[p, n_t : n_t + 16, :] = jnp.concatenate([e1[p * part : (p + 1) * part, :], totals, fill], axis=0)


def total_of(ref, start, rows):
    total = ref[0, start : start + rows, :]
    for p in range(1, ref.shape[0]):
        total = total + ref[p, start : start + rows, :]
    return total


def student_kernel(nz, nx, own, n_t, n_s, ex1, s_half, uh_ref, late, out, token, scale, prob_scr):
    token[...] = jnp.zeros_like(token)
    scale[...] = spread(GRAD_GAIN / total_of(ex1, n_t, 16)[10 : 10 + n_s])
    shape = (nz * own, BOT)
    row = lax.broadcasted_iota(jnp.int32, shape, 0)
    lane = lax.broadcasted_iota(jnp.int32, shape, 1)
    base = lax.axis_index("x") * own
    pick = jnp.zeros(shape, jnp.bool_)
    for i in range(own):
        for z in range(nz):
            pick = pick | ((row == i * nz + z) & (lane == z * nx * own + base + i))
    picked = mm(jnp.where(pick, 1.0, 0.0).astype(BF16), s_half[...], 1, 1).astype(BF16)
    n_c = uh_ref.shape[1] // 128
    per = (own + 1) * n_c

    def step(j, carry):
        uh = uh_ref[:, pl.ds(pl.multiple_of(j * CB, CB), CB)]
        dots = jnp.zeros((8, CB), F32)
        for r in range(s_half.shape[0] // 128):
            rows = slice(r * 128, (r + 1) * 128)
            logits = mm(s_half[rows, :], uh, 1, 0)
            prob = jnp.exp2(logits * STUD_GAIN) * jnp.concatenate([scale[rows, :]] * (CB // 128), axis=1)
            dots = dots + jnp.sum((prob * logits).reshape(16, 8, CB), axis=0)
            prob_scr[rows, :] = prob.astype(BF16)
        d = mm(picked, prob_scr[...], 1, 0)
        dot_row = jnp.broadcast_to(jnp.sum(dots, axis=0, keepdims=True), (nz, CB))
        for k in range(CB // 128):
            lanes = slice(k * 128, (k + 1) * 128)
            at = j * (CB // 128) + k
            for i in range(own):
                out[pl.ds(i * n_c + at, nz, stride=per), :] = d[i * nz : (i + 1) * nz, lanes]
            out[pl.ds(own * n_c + at, nz, stride=per), :] = dot_row[:, lanes]
        return carry

    lax.fori_loop(0, uh_ref.shape[1] // CB, step, 0)


def pass2_kernel(n_t, ex1, t2, uh_ref, token, pay, log_a, scr, acc, gain):
    la = jnp.log(total_of(ex1, 0, n_t)) * -LOG2E
    log_a[...] = la
    gain[...] = spread(la)
    pay[n_t : n_t + 16, :] = total_of(ex1, n_t, 16)
    balance(t2, uh_ref, gain, scr, acc, None, None, 0)
    pay[0:n_t, :] = lane_sums(acc, n_t)


def own_rows(nz, th, g):
    z, x = lax.axis_index("z"), lax.axis_index("x")
    return [pl.multiple_of(((2 * x + c) * nz + z) * th, th) for c in range(g)]


def pass3_kernel(nz, th, n_t, ex2, log_a1, t2, uh_ref, pay, log_a2, b_out, scr, acc, gain):
    la = log_a1[...] - jnp.log(total_of(ex2, 0, n_t)) * LOG2E
    log_a2[...] = la
    gain[...] = spread(la)
    starts = own_rows(nz, th, 2)

    def finish(j, b, block, uh, t_sum):
        b_out[:, pl.ds(pl.multiple_of(j * CB, CB), CB)] = b
        mine = jnp.concatenate([block[pl.ds(s, th), :] for s in starts], axis=0) * b
        return t_sum + mm(mine.astype(BF16), uh, 1, 1)

    t_sum = balance(t2, uh_ref, gain, scr, acc, None, finish, jnp.zeros((2 * th, BOT), F32))
    pay[0:n_t, :] = lane_sums(acc, n_t)
    pay[n_t:, :] = t_sum


def final_kernel(
    nz, nx, own, th, sh, n_t, n_s,
    ex3, log_a2, b_ref, t2, uh_ref, late, other, d1, ex1, ex2, student, image, kind, norm, mine,
    gp, gs, gain, ma, s_scr, d_scr, scr,
):
    x, z = lax.axis_index("x"), lax.axis_index("z")
    peers = ex3.shape[0]
    ratio = 1.0 / total_of(ex3, 0, n_t)
    gain[...] = spread(ratio)
    s_scr[...] = spread(1.0 / total_of(ex1, n_t, 16)[10 : 10 + n_s])
    own_ratio = jnp.concatenate([gain[pl.ds(s, th), :] for s in own_rows(nz, th, 2)], axis=0)
    t_sum = total_of(ex3, n_t, 2 * th) * own_ratio
    part = 2 * sh // peers
    e1 = jnp.concatenate([ex2[p, n_t : n_t + part, :] for p in range(peers)], axis=0)
    e1 = e1 * s_scr[pl.ds(pl.multiple_of(x * 2 * sh, 2 * sh), 2 * sh), :]
    weights = selector(image[...], kind[...], 2 * th)
    dz = GRAD_GAIN * (e1 - mm(weights, t_sum, 0, 0, HI))
    s_unit, s_norm = row_unit(student[...].astype(F32))
    gs[...] = (dz - s_unit * jnp.sum(s_unit * dz, axis=1, keepdims=True)) / s_norm
    gain[...] = spread(jnp.exp2(log_a2[...]) * ratio)
    half_rows = late.shape[1]
    core = lax.axis_index("c")
    for i in range(n_t):
        g, q = (i * 128) // half_rows, (i * 128) % half_rows
        mixed = jnp.where(core == g % 2, late[g // 2, q : q + 128, :], other[g // 2, q : q + 128, :])
        ma[:, i * 128 : (i + 1) * 128] = (mixed * gain[i * 128 : (i + 1) * 128, :]).T.astype(BF16)
    total = d1[0]
    for k in range(1, nz):
        total = total + d1[k]
    d_scr[...] = total
    n_c = uh_ref.shape[1] // 128
    start = (z * nx + x) * own
    n = uh_ref.shape[1] // CB

    def fill(j, dst):
        uh = uh_ref[:, pl.ds(pl.multiple_of(j * CB, CB), CB)]
        u2 = jnp.concatenate([uh, uh], axis=0)
        for r in range(t2.shape[0] // RC):
            scr[dst, r * RC : (r + 1) * RC, :] = powers(t2, u2, None, r).astype(BF16)

    def use(j, src):
        cols = pl.ds(pl.multiple_of(j * CB, CB), CB)
        d2 = mm(ma[...], scr[src], 1, 0) * (b_ref[:, cols] * GRAD_GAIN)
        dots2 = jnp.sum(uh_ref[:, cols].astype(F32) * d2, axis=0, keepdims=True)
        row = lax.broadcasted_iota(jnp.int32, d2.shape, 0)

        def early(i):
            return jnp.concatenate(
                [d_scr[pl.ds(i * n_c + j * (CB // 128) + k, 1), :] for k in range(CB // 128)], axis=1
            )

        dots = early(own) - dots2
        outs = []
        for i in range(own):
            late = jnp.sum(jnp.where(row == start + i, d2, 0.0), axis=0, keepdims=True)
            outs.append((early(i) - late - mine[i : i + 1, cols] * dots) / norm[:, cols])
        gp[:, cols] = jnp.concatenate(outs, axis=0)

    fill(0, 0)

    def step(i, carry):
        fill(2 * i + 1, 1)
        use(2 * i, 0)
        fill(2 * i + 2, 0)
        use(2 * i + 1, 1)
        return carry

    lax.fori_loop(0, n // 2 - 1, step, 0)
    fill(n - 1, 1)
    use(n - 2, 0)
    use(n - 1, 1)


def sds(shape, dtype=F32):
    return jax.ShapeDtypeStruct(shape, dtype)


def swap(x, axes):
    return lax.all_to_all(x, axes, 0, 0, tiled=True)


def per_device(sizes, student_feat, teacher_feat, prototypes, crop_image, crop_kind):
    nz, nx, ny, nc = sizes
    peers = ny * nc
    crops, teach = student_feat.shape[0], teacher_feat.shape[0]
    th, sh = teach // 2, crops // 2
    cols = prototypes.shape[1]
    own = BOT // (nz * nx)
    teachers, gathered = teach * nz * nx, crops * nx
    n_t, n_s = teachers // 128, gathered // 128
    image, kind = crop_image.reshape(1, crops), crop_kind.reshape(1, crops)
    fl = 2 * teachers * cols * 256

    zp, sp = call(
        functools.partial(prep_kernel, nz),
        (sds((nz, 2 * th, BOT)), sds((sh, BOT))),
        student_feat,
        teacher_feat,
        image,
        kind,
        limit=58 * 1024 * 1024,
    )
    half, norm, mine = call(
        functools.partial(unit_kernel, own, nx),
        (sds((BOT, cols), BF16), sds((1, cols)), sds((own, cols))),
        prototypes,
        flops=fl // 2,
    )
    got = swap(zp, "z")
    near, late = call(
        functools.partial(pack_kernel, nz, nx),
        (sds((nx, nz * th + sh, BOT)), sds((nx, nz * th, BOT))),
        got,
        sp,
    )
    near = swap(near, "x")
    near_other = lax.ppermute(near, "c", [(0, 1), (1, 0)])
    late = swap(late, "x")
    late_other = lax.ppermute(late, "c", [(0, 1), (1, 0)])

    big = [pltpu.VMEM((2, teachers, CB), F32), pltpu.VMEM((teachers, 128), F32)]
    t2, s_half, pay1 = call(
        functools.partial(pass1_kernel, nz, nx, peers, th, sh),
        (sds((teachers, 256), BF16), sds((gathered, BOT), BF16), sds((peers, n_t + 16, 128))),
        near,
        near_other,
        half,
        scratch=big + [pltpu.VMEM((gathered, CB), F32), pltpu.VMEM((gathered, 128), F32)],
        flops=fl,
    )
    ex1 = swap(pay1, ("y", "c"))
    d1, token = call(
        functools.partial(student_kernel, nz, nx, own, n_t, n_s),
        (sds((nz * (own + 1) * cols // 128, 128)), sds((8, 128))),
        ex1,
        s_half,
        half,
        late,
        scratch=[pltpu.VMEM((gathered, 128), F32), pltpu.VMEM((gathered, CB), BF16)],
        flops=fl // 2,
    )
    d1 = swap(d1.reshape(nz, (own + 1) * cols // 128, 128), "z")
    pay2, log_a1 = call(
        functools.partial(pass2_kernel, n_t),
        (sds((n_t + 16, 128)), sds((n_t, 128))),
        ex1,
        t2,
        half,
        token,
        scratch=big + [pltpu.VMEM((teachers, 128), F32)],
        flops=fl // 4,
    )
    ex2 = lax.all_gather(pay2, ("y", "c"))
    pay3, log_a2, b3 = call(
        functools.partial(pass3_kernel, nz, th, n_t),
        (sds((n_t + teach, 128)), sds((n_t, 128)), sds((1, cols))),
        ex2,
        log_a1,
        t2,
        half,
        scratch=big + [pltpu.VMEM((teachers, 128), F32)],
        flops=fl // 4,
    )
    ex3 = lax.all_gather(pay3, ("y", "c"))
    return call(
        functools.partial(final_kernel, nz, nx, own, th, sh, n_t, n_s),
        (sds((own, cols)), sds((crops, BOT))),
        ex3, log_a2, b3, t2, half, late, late_other, d1, ex1, ex2, student_feat, image, kind, norm, mine,
        scratch=[
            pltpu.VMEM((teachers, 128), F32),
            pltpu.VMEM((BOT, teachers), BF16),
            pltpu.VMEM((gathered, 128), F32),
            pltpu.VMEM(((own + 1) * cols // 128, 128), F32),
            pltpu.VMEM((2, teachers, CB), BF16),
        ],
        flops=fl * 2,
    )


def build(devices):
    grid = Mesh(devices, ("z", "x", "y", "c"))
    batch, proto = ("z", "x"), ("y", "c")
    return jax.shard_map(
        functools.partial(per_device, devices.shape),
        mesh=grid,
        in_specs=(P(batch, None), P(batch, None), P(None, proto), P(batch), P(batch)),
        out_specs=(P(batch, proto), P(batch, None)),
        check_vma=False,
    )


def solution(mesh):
    return build(mesh.devices.reshape(16, 4, 8, 2))
```

```python
import functools

import jax
import jax.numpy as jnp
from jax import lax
from jax.experimental import pallas as pl
from jax.experimental.pallas import tpu as pltpu
from jax.sharding import Mesh
from jax.sharding import PartitionSpec as P

LOSS_SCALE = 16
EPS = 1e-06
LOG2E = 1.4426950408889634
TEACH_GAIN = 25.0 * LOG2E
STUD_GAIN = 10.0 * LOG2E
GRAD_GAIN = 160.0
BOT = 128
CB = 512
RC = 256
IMGS = 16
F32 = jnp.float32
BF16 = jnp.bfloat16
HI = lax.Precision.HIGHEST
VMEM_LIMIT = 16 * 1024 * 1024
INTERPRET = False


def mm(a, b, ca, cb, precision=None):
    return lax.dot_general(a, b, (((ca,), (cb,)), ((), ())), precision=precision, preferred_element_type=F32)


def call(kernel, out_shape, *args, scratch=(), flops=0, limit=VMEM_LIMIT):
    specs = pl.BlockSpec(memory_space=pltpu.VMEM)
    return pl.pallas_call(
        kernel,
        out_shape=out_shape,
        in_specs=[specs] * len(args),
        out_specs=jax.tree.map(lambda _: specs, out_shape),
        scratch_shapes=list(scratch),
        compiler_params=pltpu.CompilerParams(vmem_limit_bytes=limit),
        cost_estimate=pl.CostEstimate(flops=flops, bytes_accessed=0, transcendentals=0),
        interpret=INTERPRET,
    )(*args)


def row_unit(x):
    norm = jnp.sqrt(jnp.sum(x * x, axis=-1, keepdims=True) + EPS)
    return x / norm, norm


def selector(image, kind, teach_rows):
    shape = (teach_rows, image.shape[1])
    teach = lax.broadcasted_iota(jnp.int32, shape, 0)
    local = jnp.bitwise_and(jnp.broadcast_to(image, shape), IMGS - 1)
    kinds = jnp.broadcast_to(kind, shape)
    weight = jnp.where(kinds == 0, 0.5, jnp.where(jnp.bitwise_and(teach, 1) == 2 - kinds, 1.0, 0.0))
    return jnp.where(local == jnp.right_shift(teach, 1), weight, 0.0)


def spread(rows):
    parts = [jnp.broadcast_to(rows[i : i + 1, :], (128, 128)).T for i in range(rows.shape[0])]
    return jnp.concatenate(parts, axis=0)


def lane_sums(ref, n):
    parts = [jnp.sum(ref[i * 128 : (i + 1) * 128, :].T, axis=0, keepdims=True) for i in range(n)]
    return jnp.concatenate(parts, axis=0)


def prep_kernel(nz, student, teacher, image, kind, zp):
    s_unit = row_unit(student[...].astype(F32))[0]
    t_unit = row_unit(teacher[...].astype(F32))[0]
    weights = selector(image[...], kind[...], teacher.shape[0])
    mixed = mm(weights.astype(BF16), s_unit.astype(BF16), 1, 0)
    th = teacher.shape[0] // 2
    first = lax.axis_index("c") == 0
    t = jnp.where(first, t_unit[:th], t_unit[th:])
    m = jnp.where(first, mixed[:th], mixed[th:])
    for p in range(nz):
        zp[p, 0:th, :] = t
        zp[p, th : 2 * th, :] = m


def unit_kernel(own, nx, proto, half, norm, mine):
    start = (lax.axis_index("z") * nx + lax.axis_index("x")) * own

    def step(j, carry):
        cols = pl.ds(pl.multiple_of(j * CB, CB), CB)
        v = proto[:, cols]
        n = jnp.sqrt(jnp.sum(v * v, axis=0, keepdims=True) + EPS)
        unit = v / n
        half[:, cols] = unit.astype(BF16)
        norm[:, cols] = n
        row = lax.broadcasted_iota(jnp.int32, unit.shape, 0)
        mine[:, cols] = jnp.concatenate(
            [jnp.sum(jnp.where(row == start + i, unit, 0.0), axis=0, keepdims=True) for i in range(own)], axis=0
        )
        return carry

    lax.fori_loop(0, proto.shape[1] // CB, step, 0)


def pack_kernel(nz, nx, got, student, near, late):
    th, sh = got.shape[1] // 2, student.shape[0] // 2
    s_unit = row_unit(student[...].astype(F32))[0]
    sp = jnp.where(lax.axis_index("c") == 0, s_unit[:sh], s_unit[sh:])
    for p in range(nx):
        for z in range(nz):
            near[p, z * th : (z + 1) * th, :] = got[z, 0:th, :]
            late[p, z * th : (z + 1) * th, :] = got[z, th : 2 * th, :]
        near[p, nz * th :, :] = sp


def powers(t2, u2, gain, r):
    x = mm(t2[r * RC : (r + 1) * RC, :], u2, 1, 0)
    if gain is not None:
        x = x + jnp.concatenate([gain[r * RC : (r + 1) * RC, :]] * (CB // 128), axis=1)
    return jnp.exp2(x)


def balance(t2, uh_ref, gain, scr, acc, first, finish, carry):
    n = uh_ref.shape[1] // CB
    acc[...] = jnp.zeros_like(acc)

    def block(j):
        return uh_ref[:, pl.ds(pl.multiple_of(j * CB, CB), CB)]

    def half(j, src, dst, b, carry):
        col = jnp.zeros((8, CB), F32)
        if dst is not None:
            uh = block(j)
            u2 = jnp.concatenate([uh, uh], axis=0)
        for r in range(t2.shape[0] // RC):
            rows = slice(r * RC, (r + 1) * RC)
            if dst is not None:
                e = powers(t2, u2, gain, r)
                scr[dst, rows, :] = e
                col = col + jnp.sum(e.reshape(RC // 8, 8, CB), axis=0)
            if src is not None:
                e = scr[src, rows, :]
                total = acc[rows, :]
                for k in range(CB // 128):
                    lanes = slice(k * 128, (k + 1) * 128)
                    total = total + e[:, lanes] * b[:, lanes]
                acc[rows, :] = total
        if src is not None and finish is not None:
            carry = finish(j - 1, b, scr.at[src], block(j - 1), carry)
        if dst is not None and first is not None:
            carry = first(uh, carry)
        return 1.0 / jnp.sum(col, axis=0, keepdims=True), carry

    b, carry = half(0, None, 0, None, carry)

    def step(i, state):
        b, carry = half(2 * i + 1, 0, 1, *state)
        return half(2 * i + 2, 1, 0, b, carry)

    b, carry = lax.fori_loop(0, n // 2 - 1, step, (b, carry))
    b, carry = half(n - 1, 0, 1, b, carry)
    return half(n, 1, None, b, carry)[1]


def pass1_kernel(nz, nx, peers, th, sh, near, other, uh_ref, t2, s_half, pay, scr, acc, es_scr, s_acc):
    rows_t = nz * th
    core = lax.axis_index("c")
    for g in range(2 * nx):
        both = jnp.where(core == g % 2, near[g // 2], other[g // 2])
        t = both[:rows_t].astype(BF16).astype(F32) * TEACH_GAIN
        hi = t.astype(BF16)
        t2[g * rows_t : (g + 1) * rows_t, 0:BOT] = hi
        t2[g * rows_t : (g + 1) * rows_t, BOT : 2 * BOT] = (t - hi.astype(F32)).astype(BF16)
        s_half[g * sh : (g + 1) * sh, :] = both[rows_t:].astype(BF16)
    s_acc[...] = jnp.zeros_like(s_acc)
    n_t, n_s = t2.shape[0] // 128, s_half.shape[0] // 128
    own = pl.multiple_of(lax.axis_index("x") * 2 * sh, 2 * sh)

    def first(uh, e1):
        for r in range(s_half.shape[0] // 128):
            rows = slice(r * 128, (r + 1) * 128)
            es = jnp.exp2(mm(s_half[rows, :], uh, 1, 0) * STUD_GAIN)
            es_scr[rows, :] = es
            s_acc[rows, :] += sum(es[:, k * 128 : (k + 1) * 128] for k in range(CB // 128))
        return e1 + mm(es_scr[pl.ds(own, 2 * sh), :].astype(BF16), uh, 1, 1)

    e1 = balance(t2, uh_ref, None, scr, acc, first, None, jnp.zeros((2 * sh, BOT), F32))
    sums = lane_sums(acc, n_t)
    totals = lane_sums(s_acc, n_s)
    part = 2 * sh // peers
    fill = jnp.zeros((16 - part - n_s, BOT), F32)
    for p in range(peers):
        pay[p, 0:n_t, :] = sums
        pay[p, n_t : n_t + 16, :] = jnp.concatenate([e1[p * part : (p + 1) * part, :], totals, fill], axis=0)


def total_of(ref, start, rows):
    total = ref[0, start : start + rows, :]
    for p in range(1, ref.shape[0]):
        total = total + ref[p, start : start + rows, :]
    return total


def student_kernel(nz, nx, own, n_t, n_s, ex1, s_half, uh_ref, late, log_a1, out, token, scale, prob_scr):
    token[...] = jnp.zeros_like(token)
    scale[...] = spread(GRAD_GAIN / total_of(ex1, n_t, 16)[10 : 10 + n_s])
    shape = (nz * own, BOT)
    row = lax.broadcasted_iota(jnp.int32, shape, 0)
    lane = lax.broadcasted_iota(jnp.int32, shape, 1)
    base = lax.axis_index("x") * own
    pick = jnp.zeros(shape, jnp.bool_)
    for i in range(own):
        for z in range(nz):
            pick = pick | ((row == i * nz + z) & (lane == z * nx * own + base + i))
    picked = mm(jnp.where(pick, 1.0, 0.0).astype(BF16), s_half[...], 1, 1).astype(BF16)
    n_c = uh_ref.shape[1] // 128
    per = (own + 1) * n_c

    def step(j, carry):
        uh = uh_ref[:, pl.ds(pl.multiple_of(j * CB, CB), CB)]
        dots = jnp.zeros((8, CB), F32)
        for r in range(s_half.shape[0] // 128):
            rows = slice(r * 128, (r + 1) * 128)
            logits = mm(s_half[rows, :], uh, 1, 0)
            prob = jnp.exp2(logits * STUD_GAIN) * jnp.concatenate([scale[rows, :]] * (CB // 128), axis=1)
            dots = dots + jnp.sum((prob * logits).reshape(16, 8, CB), axis=0)
            prob_scr[rows, :] = prob.astype(BF16)
        d = mm(picked, prob_scr[...], 1, 0)
        dot_row = jnp.broadcast_to(jnp.sum(dots, axis=0, keepdims=True), (nz, CB))
        for k in range(CB // 128):
            lanes = slice(k * 128, (k + 1) * 128)
            at = j * (CB // 128) + k
            for i in range(own):
                out[pl.ds(i * n_c + at, nz, stride=per), :] = d[i * nz : (i + 1) * nz, lanes]
            out[pl.ds(own * n_c + at, nz, stride=per), :] = dot_row[:, lanes]
        return carry

    lax.fori_loop(0, uh_ref.shape[1] // CB, step, 0)


def pass2_kernel(peers, n_t, ex1, t2, uh_ref, pay, log_a, scr, acc, gain):
    la = jnp.log(total_of(ex1, 0, n_t)) * -LOG2E
    log_a[...] = la
    gain[...] = spread(la)
    e1 = total_of(ex1, n_t, 16)
    balance(t2, uh_ref, gain, scr, acc, None, None, 0)
    sums = lane_sums(acc, n_t)
    for p in range(peers):
        pay[p, 0:n_t, :] = sums
        pay[p, n_t : n_t + 16, :] = e1


def own_rows(nz, th, g):
    z, x = lax.axis_index("z"), lax.axis_index("x")
    return [pl.multiple_of(((2 * x + c) * nz + z) * th, th) for c in range(g)]


def pass3_kernel(nz, th, n_t, ex2, log_a1, t2, uh_ref, token, pay, log_a2, b_out, scr, acc, gain):
    la = log_a1[...] - jnp.log(total_of(ex2, 0, n_t)) * LOG2E
    log_a2[...] = la
    gain[...] = spread(la)
    starts = own_rows(nz, th, 2)

    def finish(j, b, block, uh, t_sum):
        b_out[:, pl.ds(pl.multiple_of(j * CB, CB), CB)] = b
        mine = jnp.concatenate([block[pl.ds(s, th), :] for s in starts], axis=0) * b
        return t_sum + mm(mine.astype(BF16), uh, 1, 1)

    t_sum = balance(t2, uh_ref, gain, scr, acc, None, finish, jnp.zeros((2 * th, BOT), F32))
    pay[0:n_t, :] = lane_sums(acc, n_t)
    pay[n_t:, :] = t_sum


def final_kernel(
    nz, nx, own, th, sh, n_t, n_s,
    ex3, log_a2, b_ref, t2, uh_ref, late, other, ex1, ex2, student, image, kind,
    d2_out, gs, gain, ma, s_scr, scr,
):
    x, z = lax.axis_index("x"), lax.axis_index("z")
    peers = ex3.shape[0]
    ratio = 1.0 / total_of(ex3, 0, n_t)
    gain[...] = spread(ratio)
    s_scr[...] = spread(1.0 / total_of(ex1, n_t, 16)[10 : 10 + n_s])
    own_ratio = jnp.concatenate([gain[pl.ds(s, th), :] for s in own_rows(nz, th, 2)], axis=0)
    t_sum = total_of(ex3, n_t, 2 * th) * own_ratio
    part = 2 * sh // peers
    e1 = jnp.concatenate([ex2[p, n_t : n_t + part, :] for p in range(peers)], axis=0)
    e1 = e1 * s_scr[pl.ds(pl.multiple_of(x * 2 * sh, 2 * sh), 2 * sh), :]
    weights = selector(image[...], kind[...], 2 * th)
    dz = GRAD_GAIN * (e1 - mm(weights, t_sum, 0, 0, HI))
    s_unit, s_norm = row_unit(student[...].astype(F32))
    gs[...] = (dz - s_unit * jnp.sum(s_unit * dz, axis=1, keepdims=True)) / s_norm
    gain[...] = spread(jnp.exp2(log_a2[...]) * ratio)
    half_rows = late.shape[1]
    core = lax.axis_index("c")
    for i in range(n_t):
        g, q = (i * 128) // half_rows, (i * 128) % half_rows
        mixed = jnp.where(core == g % 2, late[g // 2, q : q + 128, :], other[g // 2, q : q + 128, :])
        ma[:, i * 128 : (i + 1) * 128] = (mixed * gain[i * 128 : (i + 1) * 128, :]).T.astype(BF16)
    start = (z * nx + x) * own
    n = uh_ref.shape[1] // CB

    def fill(j, dst):
        uh = uh_ref[:, pl.ds(pl.multiple_of(j * CB, CB), CB)]
        u2 = jnp.concatenate([uh, uh], axis=0)
        for r in range(t2.shape[0] // RC):
            scr[dst, r * RC : (r + 1) * RC, :] = powers(t2, u2, None, r).astype(BF16)

    def use(j, src):
        cols = pl.ds(pl.multiple_of(j * CB, CB), CB)
        d2 = mm(ma[...], scr[src], 1, 0) * (b_ref[:, cols] * GRAD_GAIN)
        dots2 = jnp.sum(uh_ref[:, cols].astype(F32) * d2, axis=0, keepdims=True)
        row = lax.broadcasted_iota(jnp.int32, d2.shape, 0)

        outs = [jnp.sum(jnp.where(row == start + i, d2, 0.0), axis=0, keepdims=True) for i in range(own)]
        d2_out[:, cols] = jnp.concatenate(outs + [dots2], axis=0)

    fill(0, 0)

    def step(i, carry):
        fill(2 * i + 1, 1)
        use(2 * i, 0)
        fill(2 * i + 2, 0)
        use(2 * i + 1, 1)
        return carry

    lax.fori_loop(0, n // 2 - 1, step, 0)
    fill(n - 1, 1)
    use(n - 2, 0)
    use(n - 1, 1)


def join_kernel(own, d1, d2, norm, mine, gp, d_scr):
    total = d1[0]
    for k in range(1, d1.shape[0]):
        total = total + d1[k]
    d_scr[...] = total
    n_c = norm.shape[1] // 128
    for k in range(n_c):
        cols = slice(k * 128, (k + 1) * 128)
        dots = d_scr[own * n_c + k : own * n_c + k + 1, :] - d2[own : own + 1, cols]
        early = jnp.concatenate([d_scr[i * n_c + k : i * n_c + k + 1, :] for i in range(own)], axis=0)
        gp[:, cols] = (early - d2[0:own, cols] - mine[:, cols] * dots) / norm[:, cols]


def sds(shape, dtype=F32):
    return jax.ShapeDtypeStruct(shape, dtype)


def swap(x, axes):
    return lax.all_to_all(x, axes, 0, 0, tiled=True)


def per_device(sizes, student_feat, teacher_feat, prototypes, crop_image, crop_kind):
    nz, nx, ny, nc = sizes
    peers = ny * nc
    crops, teach = student_feat.shape[0], teacher_feat.shape[0]
    th, sh = teach // 2, crops // 2
    cols = prototypes.shape[1]
    own = BOT // (nz * nx)
    teachers, gathered = teach * nz * nx, crops * nx
    n_t, n_s = teachers // 128, gathered // 128
    image, kind = crop_image.reshape(1, crops), crop_kind.reshape(1, crops)
    fl = 2 * teachers * cols * 256

    zp = call(
        functools.partial(prep_kernel, nz),
        sds((nz, 2 * th, BOT)),
        student_feat,
        teacher_feat,
        image,
        kind,
        limit=58 * 1024 * 1024,
    )
    half, norm, mine = call(
        functools.partial(unit_kernel, own, nx),
        (sds((BOT, cols), BF16), sds((1, cols)), sds((own, cols))),
        prototypes,
        flops=fl // 2,
    )
    got = swap(zp, "z")
    near, late = call(
        functools.partial(pack_kernel, nz, nx),
        (sds((nx, nz * th + sh, BOT)), sds((nx, nz * th, BOT))),
        got,
        student_feat,
    )
    near = swap(near, "x")
    near_other = lax.ppermute(near, "c", [(0, 1), (1, 0)])
    late = swap(late, "x")
    late_other = lax.ppermute(late, "c", [(0, 1), (1, 0)])

    big = [pltpu.VMEM((2, teachers, CB), F32), pltpu.VMEM((teachers, 128), F32)]
    t2, s_half, pay1 = call(
        functools.partial(pass1_kernel, nz, nx, peers, th, sh),
        (sds((teachers, 256), BF16), sds((gathered, BOT), BF16), sds((peers, n_t + 16, 128))),
        near,
        near_other,
        half,
        scratch=big + [pltpu.VMEM((gathered, CB), F32), pltpu.VMEM((gathered, 128), F32)],
        flops=fl,
    )
    ex1 = swap(pay1, ("y", "c"))
    pay2, log_a1 = call(
        functools.partial(pass2_kernel, peers, n_t),
        (sds((peers, n_t + 16, 128)), sds((n_t, 128))),
        ex1,
        t2,
        half,
        scratch=big + [pltpu.VMEM((teachers, 128), F32)],
        flops=fl // 4,
    )
    ex2 = swap(pay2, ("y", "c"))
    d1, token = call(
        functools.partial(student_kernel, nz, nx, own, n_t, n_s),
        (sds((nz * (own + 1) * cols // 128, 128)), sds((8, 128))),
        ex1,
        s_half,
        half,
        late,
        log_a1,
        scratch=[pltpu.VMEM((gathered, 128), F32), pltpu.VMEM((gathered, CB), BF16)],
        flops=fl // 2,
    )
    d1 = swap(d1.reshape(nz, (own + 1) * cols // 128, 128), "z")
    pay3, log_a2, b3 = call(
        functools.partial(pass3_kernel, nz, th, n_t),
        (sds((n_t + teach, 128)), sds((n_t, 128)), sds((1, cols))),
        ex2,
        log_a1,
        t2,
        half,
        token,
        scratch=big + [pltpu.VMEM((teachers, 128), F32)],
        flops=fl // 4,
    )
    ex3 = lax.all_gather(pay3, ("y", "c"))
    d2, grad_student = call(
        functools.partial(final_kernel, nz, nx, own, th, sh, n_t, n_s),
        (sds((own + 1, cols)), sds((crops, BOT))),
        ex3, log_a2, b3, t2, half, late, late_other, ex1, ex2, student_feat, image, kind,
        scratch=[
            pltpu.VMEM((teachers, 128), F32),
            pltpu.VMEM((BOT, teachers), BF16),
            pltpu.VMEM((gathered, 128), F32),
            pltpu.VMEM((2, teachers, CB), BF16),
        ],
        flops=fl * 2,
    )
    grad_proto = call(
        functools.partial(join_kernel, own),
        sds((own, cols)),
        d1,
        d2,
        norm,
        mine,
        scratch=[pltpu.VMEM(((own + 1) * cols // 128, 128), F32)],
    )
    return grad_proto, grad_student


def build(devices):
    grid = Mesh(devices, ("z", "x", "y", "c"))
    batch, proto = ("z", "x"), ("y", "c")
    return jax.shard_map(
        functools.partial(per_device, devices.shape),
        mesh=grid,
        in_specs=(P(batch, None), P(batch, None), P(None, proto), P(batch), P(batch)),
        out_specs=(P(batch, proto), P(batch, None)),
        check_vma=False,
    )


def solution(mesh):
    return build(mesh.devices.reshape(16, 4, 8, 2))
```

```python
import functools

import jax
import jax.numpy as jnp
from jax import lax
from jax.experimental import pallas as pl
from jax.experimental.pallas import tpu as pltpu
from jax.sharding import Mesh
from jax.sharding import PartitionSpec as P

LOSS_SCALE = 16
EPS = 1e-06
LOG2E = 1.4426950408889634
TEACH_GAIN = 25.0 * LOG2E
STUD_GAIN = 10.0 * LOG2E
GRAD_GAIN = 160.0
BOT = 128
CB = 512
RC = 256
IMGS = 16
F32 = jnp.float32
BF16 = jnp.bfloat16
HI = lax.Precision.HIGHEST
VMEM_LIMIT = 16 * 1024 * 1024
INTERPRET = False


def mm(a, b, ca, cb, precision=None):
    return lax.dot_general(a, b, (((ca,), (cb,)), ((), ())), precision=precision, preferred_element_type=F32)


def call(kernel, out_shape, *args, scratch=(), flops=0, limit=VMEM_LIMIT):
    specs = pl.BlockSpec(memory_space=pltpu.VMEM)
    return pl.pallas_call(
        kernel,
        out_shape=out_shape,
        in_specs=[specs] * len(args),
        out_specs=jax.tree.map(lambda _: specs, out_shape),
        scratch_shapes=list(scratch),
        compiler_params=pltpu.CompilerParams(vmem_limit_bytes=limit),
        cost_estimate=pl.CostEstimate(flops=flops, bytes_accessed=0, transcendentals=0),
        interpret=INTERPRET,
    )(*args)


def row_unit(x):
    norm = jnp.sqrt(jnp.sum(x * x, axis=-1, keepdims=True) + EPS)
    return x / norm, norm


def selector(image, kind, teach_rows):
    shape = (teach_rows, image.shape[1])
    teach = lax.broadcasted_iota(jnp.int32, shape, 0)
    local = jnp.bitwise_and(jnp.broadcast_to(image, shape), IMGS - 1)
    kinds = jnp.broadcast_to(kind, shape)
    weight = jnp.where(kinds == 0, 0.5, jnp.where(jnp.bitwise_and(teach, 1) == 2 - kinds, 1.0, 0.0))
    return jnp.where(local == jnp.right_shift(teach, 1), weight, 0.0)


def spread(rows):
    parts = [jnp.broadcast_to(rows[i : i + 1, :], (128, 128)).T for i in range(rows.shape[0])]
    return jnp.concatenate(parts, axis=0)


def lane_sums(ref, n):
    parts = [jnp.sum(ref[i * 128 : (i + 1) * 128, :].T, axis=0, keepdims=True) for i in range(n)]
    return jnp.concatenate(parts, axis=0)


def prep_kernel(nz, student, teacher, image, kind, zp):
    s_unit = row_unit(student[...].astype(F32))[0]
    t_unit = row_unit(teacher[...].astype(F32))[0]
    weights = selector(image[...], kind[...], teacher.shape[0])
    mixed = mm(weights.astype(BF16), s_unit.astype(BF16), 1, 0)
    th = teacher.shape[0] // 2
    first = lax.axis_index("c") == 0
    t = jnp.where(first, t_unit[:th], t_unit[th:])
    m = jnp.where(first, mixed[:th], mixed[th:])
    for p in range(nz):
        zp[p, 0:th, :] = t
        zp[p, th : 2 * th, :] = m


def unit_kernel(own, nx, proto, half, norm, mine):
    start = (lax.axis_index("z") * nx + lax.axis_index("x")) * own

    def step(j, carry):
        cols = pl.ds(pl.multiple_of(j * CB, CB), CB)
        v = proto[:, cols]
        n = jnp.sqrt(jnp.sum(v * v, axis=0, keepdims=True) + EPS)
        unit = v / n
        half[:, cols] = unit.astype(BF16)
        norm[:, cols] = n
        row = lax.broadcasted_iota(jnp.int32, unit.shape, 0)
        mine[:, cols] = jnp.concatenate(
            [jnp.sum(jnp.where(row == start + i, unit, 0.0), axis=0, keepdims=True) for i in range(own)], axis=0
        )
        return carry

    lax.fori_loop(0, proto.shape[1] // CB, step, 0)


def pack_kernel(nz, nx, got, student, near):
    th, sh = got.shape[1] // 2, student.shape[0] // 2
    s_unit = row_unit(student[...].astype(F32))[0]
    sp = jnp.where(lax.axis_index("c") == 0, s_unit[:sh], s_unit[sh:])
    for p in range(nx):
        for z in range(nz):
            near[p, z * th : (z + 1) * th, :] = got[z, 0:th, :]
            near[p, (nz + z) * th : (nz + z + 1) * th, :] = got[z, th : 2 * th, :]
        near[p, 2 * nz * th :, :] = sp


def powers(t2, u2, gain, r):
    x = mm(t2[r * RC : (r + 1) * RC, :], u2, 1, 0)
    if gain is not None:
        x = x + jnp.concatenate([gain[r * RC : (r + 1) * RC, :]] * (CB // 128), axis=1)
    return jnp.exp2(x)


def balance(t2, uh_ref, gain, scr, acc, first, finish, carry):
    n = uh_ref.shape[1] // CB
    acc[...] = jnp.zeros_like(acc)

    def block(j):
        return uh_ref[:, pl.ds(pl.multiple_of(j * CB, CB), CB)]

    def half(j, src, dst, b, carry):
        col = jnp.zeros((8, CB), F32)
        if dst is not None:
            uh = block(j)
            u2 = jnp.concatenate([uh, uh], axis=0)
        for r in range(t2.shape[0] // RC):
            rows = slice(r * RC, (r + 1) * RC)
            if dst is not None:
                e = powers(t2, u2, gain, r)
                scr[dst, rows, :] = e
                col = col + jnp.sum(e.reshape(RC // 8, 8, CB), axis=0)
            if src is not None:
                e = scr[src, rows, :]
                total = acc[rows, :]
                for k in range(CB // 128):
                    lanes = slice(k * 128, (k + 1) * 128)
                    total = total + e[:, lanes] * b[:, lanes]
                acc[rows, :] = total
        if src is not None and finish is not None:
            carry = finish(j - 1, b, scr.at[src], block(j - 1), carry)
        if dst is not None and first is not None:
            carry = first(uh, carry)
        return 1.0 / jnp.sum(col, axis=0, keepdims=True), carry

    b, carry = half(0, None, 0, None, carry)

    def step(i, state):
        b, carry = half(2 * i + 1, 0, 1, *state)
        return half(2 * i + 2, 1, 0, b, carry)

    b, carry = lax.fori_loop(0, n // 2 - 1, step, (b, carry))
    b, carry = half(n - 1, 0, 1, b, carry)
    return half(n, 1, None, b, carry)[1]


def pass1_kernel(nz, nx, peers, th, sh, near, other, uh_ref, t2, s_half, mixed, pay, scr, acc, es_scr, s_acc):
    rows_t = nz * th
    core = lax.axis_index("c")
    for g in range(2 * nx):
        both = jnp.where(core == g % 2, near[g // 2], other[g // 2])
        t = both[:rows_t].astype(BF16).astype(F32) * TEACH_GAIN
        hi = t.astype(BF16)
        t2[g * rows_t : (g + 1) * rows_t, 0:BOT] = hi
        t2[g * rows_t : (g + 1) * rows_t, BOT : 2 * BOT] = (t - hi.astype(F32)).astype(BF16)
        mixed[g * rows_t : (g + 1) * rows_t, :] = both[rows_t : 2 * rows_t]
        s_half[g * sh : (g + 1) * sh, :] = both[2 * rows_t :].astype(BF16)
    s_acc[...] = jnp.zeros_like(s_acc)
    n_t, n_s = t2.shape[0] // 128, s_half.shape[0] // 128
    own = pl.multiple_of(lax.axis_index("x") * 2 * sh, 2 * sh)

    def first(uh, e1):
        for r in range(s_half.shape[0] // 128):
            rows = slice(r * 128, (r + 1) * 128)
            es = jnp.exp2(mm(s_half[rows, :], uh, 1, 0) * STUD_GAIN)
            es_scr[rows, :] = es
            s_acc[rows, :] += sum(es[:, k * 128 : (k + 1) * 128] for k in range(CB // 128))
        return e1 + mm(es_scr[pl.ds(own, 2 * sh), :].astype(BF16), uh, 1, 1)

    e1 = balance(t2, uh_ref, None, scr, acc, first, None, jnp.zeros((2 * sh, BOT), F32))
    sums = lane_sums(acc, n_t)
    totals = lane_sums(s_acc, n_s)
    part = 2 * sh // peers
    fill = jnp.zeros((16 - part - n_s, BOT), F32)
    for p in range(peers):
        pay[p, 0:n_t, :] = sums
        pay[p, n_t : n_t + 16, :] = jnp.concatenate([e1[p * part : (p + 1) * part, :], totals, fill], axis=0)


def total_of(ref, start, rows):
    total = ref[0, start : start + rows, :]
    for p in range(1, ref.shape[0]):
        total = total + ref[p, start : start + rows, :]
    return total


def student_kernel(nz, nx, own, n_t, n_s, ex1, s_half, uh_ref, log_a1, out, token, scale, prob_scr):
    token[...] = jnp.zeros_like(token)
    scale[...] = spread(GRAD_GAIN / total_of(ex1, n_t, 16)[10 : 10 + n_s])
    shape = (nz * own, BOT)
    row = lax.broadcasted_iota(jnp.int32, shape, 0)
    lane = lax.broadcasted_iota(jnp.int32, shape, 1)
    base = lax.axis_index("x") * own
    pick = jnp.zeros(shape, jnp.bool_)
    for i in range(own):
        for z in range(nz):
            pick = pick | ((row == i * nz + z) & (lane == z * nx * own + base + i))
    picked = mm(jnp.where(pick, 1.0, 0.0).astype(BF16), s_half[...], 1, 1).astype(BF16)
    n_c = uh_ref.shape[1] // 128
    per = (own + 1) * n_c

    def step(j, carry):
        uh = uh_ref[:, pl.ds(pl.multiple_of(j * CB, CB), CB)]
        dots = jnp.zeros((8, CB), F32)
        for r in range(s_half.shape[0] // 128):
            rows = slice(r * 128, (r + 1) * 128)
            logits = mm(s_half[rows, :], uh, 1, 0)
            prob = jnp.exp2(logits * STUD_GAIN) * jnp.concatenate([scale[rows, :]] * (CB // 128), axis=1)
            dots = dots + jnp.sum((prob * logits).reshape(16, 8, CB), axis=0)
            prob_scr[rows, :] = prob.astype(BF16)
        d = mm(picked, prob_scr[...], 1, 0)
        dot_row = jnp.broadcast_to(jnp.sum(dots, axis=0, keepdims=True), (nz, CB))
        for k in range(CB // 128):
            lanes = slice(k * 128, (k + 1) * 128)
            at = j * (CB // 128) + k
            for i in range(own):
                out[pl.ds(i * n_c + at, nz, stride=per), :] = d[i * nz : (i + 1) * nz, lanes]
            out[pl.ds(own * n_c + at, nz, stride=per), :] = dot_row[:, lanes]
        return carry

    lax.fori_loop(0, uh_ref.shape[1] // CB, step, 0)


def pass2_kernel(peers, n_t, ex1, t2, uh_ref, pay, log_a, scr, acc, gain):
    la = jnp.log(total_of(ex1, 0, n_t)) * -LOG2E
    log_a[...] = la
    gain[...] = spread(la)
    e1 = total_of(ex1, n_t, 16)
    balance(t2, uh_ref, gain, scr, acc, None, None, 0)
    sums = lane_sums(acc, n_t)
    for p in range(peers):
        pay[p, 0:n_t, :] = sums
        pay[p, n_t : n_t + 16, :] = e1


def own_rows(nz, th, g):
    z, x = lax.axis_index("z"), lax.axis_index("x")
    return [pl.multiple_of(((2 * x + c) * nz + z) * th, th) for c in range(g)]


def pass3_kernel(nz, th, n_t, ex2, log_a1, t2, uh_ref, token, pay, log_a2, b_out, scr, acc, gain):
    la = log_a1[...] - jnp.log(total_of(ex2, 0, n_t)) * LOG2E
    log_a2[...] = la
    gain[...] = spread(la)
    starts = own_rows(nz, th, 2)

    def finish(j, b, block, uh, t_sum):
        b_out[:, pl.ds(pl.multiple_of(j * CB, CB), CB)] = b
        mine = jnp.concatenate([block[pl.ds(s, th), :] for s in starts], axis=0) * b
        return t_sum + mm(mine.astype(BF16), uh, 1, 1)

    t_sum = balance(t2, uh_ref, gain, scr, acc, None, finish, jnp.zeros((2 * th, BOT), F32))
    pay[0:n_t, :] = lane_sums(acc, n_t)
    pay[n_t:, :] = t_sum


def final_kernel(
    nz, nx, own, th, sh, n_t, n_s,
    ex3, log_a2, b_ref, t2, uh_ref, mixed, ex1, ex2, student, image, kind,
    d2_out, gs, gain, ma, s_scr, scr,
):
    x, z = lax.axis_index("x"), lax.axis_index("z")
    peers = ex3.shape[0]
    ratio = 1.0 / total_of(ex3, 0, n_t)
    gain[...] = spread(ratio)
    s_scr[...] = spread(1.0 / total_of(ex1, n_t, 16)[10 : 10 + n_s])
    own_ratio = jnp.concatenate([gain[pl.ds(s, th), :] for s in own_rows(nz, th, 2)], axis=0)
    t_sum = total_of(ex3, n_t, 2 * th) * own_ratio
    part = 2 * sh // peers
    e1 = jnp.concatenate([ex2[p, n_t : n_t + part, :] for p in range(peers)], axis=0)
    e1 = e1 * s_scr[pl.ds(pl.multiple_of(x * 2 * sh, 2 * sh), 2 * sh), :]
    weights = selector(image[...], kind[...], 2 * th)
    dz = GRAD_GAIN * (e1 - mm(weights, t_sum, 0, 0, HI))
    s_unit, s_norm = row_unit(student[...].astype(F32))
    gs[...] = (dz - s_unit * jnp.sum(s_unit * dz, axis=1, keepdims=True)) / s_norm
    gain[...] = spread(jnp.exp2(log_a2[...]) * ratio)
    for i in range(n_t):
        rows = slice(i * 128, (i + 1) * 128)
        ma[:, rows] = (mixed[rows, :] * gain[rows, :]).T.astype(BF16)
    start = (z * nx + x) * own
    n = uh_ref.shape[1] // CB

    def fill(j, dst):
        uh = uh_ref[:, pl.ds(pl.multiple_of(j * CB, CB), CB)]
        u2 = jnp.concatenate([uh, uh], axis=0)
        for r in range(t2.shape[0] // RC):
            scr[dst, r * RC : (r + 1) * RC, :] = powers(t2, u2, None, r).astype(BF16)

    def use(j, src):
        cols = pl.ds(pl.multiple_of(j * CB, CB), CB)
        d2 = mm(ma[...], scr[src], 1, 0) * (b_ref[:, cols] * GRAD_GAIN)
        dots2 = jnp.sum(uh_ref[:, cols].astype(F32) * d2, axis=0, keepdims=True)
        row = lax.broadcasted_iota(jnp.int32, d2.shape, 0)

        outs = [jnp.sum(jnp.where(row == start + i, d2, 0.0), axis=0, keepdims=True) for i in range(own)]
        d2_out[:, cols] = jnp.concatenate(outs + [dots2], axis=0)

    fill(0, 0)

    def step(i, carry):
        fill(2 * i + 1, 1)
        use(2 * i, 0)
        fill(2 * i + 2, 0)
        use(2 * i + 1, 1)
        return carry

    lax.fori_loop(0, n // 2 - 1, step, 0)
    fill(n - 1, 1)
    use(n - 2, 0)
    use(n - 1, 1)


def join_kernel(own, d1, d2, norm, mine, gp, d_scr):
    total = d1[0]
    for k in range(1, d1.shape[0]):
        total = total + d1[k]
    d_scr[...] = total
    n_c = norm.shape[1] // 128
    for k in range(n_c):
        cols = slice(k * 128, (k + 1) * 128)
        dots = d_scr[own * n_c + k : own * n_c + k + 1, :] - d2[own : own + 1, cols]
        early = jnp.concatenate([d_scr[i * n_c + k : i * n_c + k + 1, :] for i in range(own)], axis=0)
        gp[:, cols] = (early - d2[0:own, cols] - mine[:, cols] * dots) / norm[:, cols]


def sds(shape, dtype=F32):
    return jax.ShapeDtypeStruct(shape, dtype)


def swap(x, axes):
    return lax.all_to_all(x, axes, 0, 0, tiled=True)


def per_device(sizes, student_feat, teacher_feat, prototypes, crop_image, crop_kind):
    nz, nx, ny, nc = sizes
    peers = ny * nc
    crops, teach = student_feat.shape[0], teacher_feat.shape[0]
    th, sh = teach // 2, crops // 2
    cols = prototypes.shape[1]
    own = BOT // (nz * nx)
    teachers, gathered = teach * nz * nx, crops * nx
    n_t, n_s = teachers // 128, gathered // 128
    image, kind = crop_image.reshape(1, crops), crop_kind.reshape(1, crops)
    fl = 2 * teachers * cols * 256

    zp = call(
        functools.partial(prep_kernel, nz),
        sds((nz, 2 * th, BOT)),
        student_feat,
        teacher_feat,
        image,
        kind,
        limit=58 * 1024 * 1024,
    )
    half, norm, mine = call(
        functools.partial(unit_kernel, own, nx),
        (sds((BOT, cols), BF16), sds((1, cols)), sds((own, cols))),
        prototypes,
        flops=fl // 2,
    )
    got = swap(zp, "z")
    near = call(
        functools.partial(pack_kernel, nz, nx),
        sds((nx, 2 * nz * th + sh, BOT)),
        got,
        student_feat,
    )
    near = swap(near, "x")
    other = lax.ppermute(near, "c", [(0, 1), (1, 0)])

    big = [pltpu.VMEM((2, teachers, CB), F32), pltpu.VMEM((teachers, 128), F32)]
    t2, s_half, mixed, pay1 = call(
        functools.partial(pass1_kernel, nz, nx, peers, th, sh),
        (sds((teachers, 256), BF16), sds((gathered, BOT), BF16), sds((teachers, BOT)), sds((peers, n_t + 16, 128))),
        near,
        other,
        half,
        scratch=big + [pltpu.VMEM((gathered, CB), F32), pltpu.VMEM((gathered, 128), F32)],
        flops=fl,
    )
    ex1 = swap(pay1, ("y", "c"))
    pay2, log_a1 = call(
        functools.partial(pass2_kernel, peers, n_t),
        (sds((peers, n_t + 16, 128)), sds((n_t, 128))),
        ex1,
        t2,
        half,
        scratch=big + [pltpu.VMEM((teachers, 128), F32)],
        flops=fl // 4,
    )
    ex2 = swap(pay2, ("y", "c"))
    d1, token = call(
        functools.partial(student_kernel, nz, nx, own, n_t, n_s),
        (sds((nz * (own + 1) * cols // 128, 128)), sds((8, 128))),
        ex1,
        s_half,
        half,
        log_a1,
        scratch=[pltpu.VMEM((gathered, 128), F32), pltpu.VMEM((gathered, CB), BF16)],
        flops=fl // 2,
    )
    d1 = swap(d1.reshape(nz, (own + 1) * cols // 128, 128), "z")
    pay3, log_a2, b3 = call(
        functools.partial(pass3_kernel, nz, th, n_t),
        (sds((n_t + teach, 128)), sds((n_t, 128)), sds((1, cols))),
        ex2,
        log_a1,
        t2,
        half,
        token,
        scratch=big + [pltpu.VMEM((teachers, 128), F32)],
        flops=fl // 4,
    )
    ex3 = lax.all_gather(pay3, ("y", "c"))
    d2, grad_student = call(
        functools.partial(final_kernel, nz, nx, own, th, sh, n_t, n_s),
        (sds((own + 1, cols)), sds((crops, BOT))),
        ex3, log_a2, b3, t2, half, mixed, ex1, ex2, student_feat, image, kind,
        scratch=[
            pltpu.VMEM((teachers, 128), F32),
            pltpu.VMEM((BOT, teachers), BF16),
            pltpu.VMEM((gathered, 128), F32),
            pltpu.VMEM((2, teachers, CB), BF16),
        ],
        flops=fl * 2,
    )
    grad_proto = call(
        functools.partial(join_kernel, own),
        sds((own, cols)),
        d1,
        d2,
        norm,
        mine,
        scratch=[pltpu.VMEM(((own + 1) * cols // 128, 128), F32)],
    )
    return grad_proto, grad_student


def build(devices):
    grid = Mesh(devices, ("z", "x", "y", "c"))
    batch, proto = ("z", "x"), ("y", "c")
    return jax.shard_map(
        functools.partial(per_device, devices.shape),
        mesh=grid,
        in_specs=(P(batch, None), P(batch, None), P(None, proto), P(batch), P(batch)),
        out_specs=(P(batch, proto), P(batch, None)),
        check_vma=False,
    )


def solution(mesh):
    return build(mesh.devices.reshape(16, 4, 8, 2))
```

```python
import functools

import jax
import jax.numpy as jnp
from jax import lax
from jax.experimental import pallas as pl
from jax.experimental.pallas import tpu as pltpu
from jax.sharding import Mesh
from jax.sharding import PartitionSpec as P

LOSS_SCALE = 16
EPS = 1e-06
LOG2E = 1.4426950408889634
TEACH_GAIN = 25.0 * LOG2E
STUD_GAIN = 10.0 * LOG2E
GRAD_GAIN = 160.0
BOT = 128
CB = 512
RC = 256
IMGS = 16
F32 = jnp.float32
BF16 = jnp.bfloat16
HI = lax.Precision.HIGHEST
VMEM_LIMIT = 16 * 1024 * 1024
INTERPRET = False


def mm(a, b, ca, cb, precision=None):
    return lax.dot_general(a, b, (((ca,), (cb,)), ((), ())), precision=precision, preferred_element_type=F32)


def call(kernel, out_shape, *args, scratch=(), flops=0, limit=VMEM_LIMIT):
    specs = pl.BlockSpec(memory_space=pltpu.VMEM)
    return pl.pallas_call(
        kernel,
        out_shape=out_shape,
        in_specs=[specs] * len(args),
        out_specs=jax.tree.map(lambda _: specs, out_shape),
        scratch_shapes=list(scratch),
        compiler_params=pltpu.CompilerParams(vmem_limit_bytes=limit),
        cost_estimate=pl.CostEstimate(flops=flops, bytes_accessed=0, transcendentals=0),
        interpret=INTERPRET,
    )(*args)


def row_unit(x):
    norm = jnp.sqrt(jnp.sum(x * x, axis=-1, keepdims=True) + EPS)
    return x / norm, norm


def selector(image, kind, teach_rows):
    shape = (teach_rows, image.shape[1])
    teach = lax.broadcasted_iota(jnp.int32, shape, 0)
    local = jnp.bitwise_and(jnp.broadcast_to(image, shape), IMGS - 1)
    kinds = jnp.broadcast_to(kind, shape)
    weight = jnp.where(kinds == 0, 0.5, jnp.where(jnp.bitwise_and(teach, 1) == 2 - kinds, 1.0, 0.0))
    return jnp.where(local == jnp.right_shift(teach, 1), weight, 0.0)


def spread(rows):
    parts = [jnp.broadcast_to(rows[i : i + 1, :], (128, 128)).T for i in range(rows.shape[0])]
    return jnp.concatenate(parts, axis=0)


def lane_sums(ref, n):
    parts = [jnp.sum(ref[i * 128 : (i + 1) * 128, :].T, axis=0, keepdims=True) for i in range(n)]
    return jnp.concatenate(parts, axis=0)


def prep_kernel(nz, student, teacher, image, kind, zp):
    s_unit = row_unit(student[...].astype(F32))[0]
    t_unit = row_unit(teacher[...].astype(F32))[0]
    weights = selector(image[...], kind[...], teacher.shape[0])
    mixed = mm(weights.astype(BF16), s_unit.astype(BF16), 1, 0)
    th = teacher.shape[0] // 2
    first = lax.axis_index("c") == 0
    t = jnp.where(first, t_unit[:th], t_unit[th:])
    m = jnp.where(first, mixed[:th], mixed[th:])
    for p in range(nz):
        zp[p, 0:th, :] = t
        zp[p, th : 2 * th, :] = m


def unit_kernel(own, nx, proto, half, norm, mine):
    start = (lax.axis_index("z") * nx + lax.axis_index("x")) * own

    def step(j, carry):
        cols = pl.ds(pl.multiple_of(j * CB, CB), CB)
        v = proto[:, cols]
        n = jnp.sqrt(jnp.sum(v * v, axis=0, keepdims=True) + EPS)
        unit = v / n
        half[:, cols] = unit.astype(BF16)
        norm[:, cols] = n
        row = lax.broadcasted_iota(jnp.int32, unit.shape, 0)
        mine[:, cols] = jnp.concatenate(
            [jnp.sum(jnp.where(row == start + i, unit, 0.0), axis=0, keepdims=True) for i in range(own)], axis=0
        )
        return carry

    lax.fori_loop(0, proto.shape[1] // CB, step, 0)


def pack_kernel(nz, nx, got, student, near):
    th, sh = got.shape[1] // 2, student.shape[0] // 2
    s_unit = row_unit(student[...].astype(F32))[0]
    sp = jnp.where(lax.axis_index("c") == 0, s_unit[:sh], s_unit[sh:])
    for p in range(nx):
        for z in range(nz):
            near[p, z * th : (z + 1) * th, :] = got[z, 0:th, :]
            near[p, (nz + z) * th : (nz + z + 1) * th, :] = got[z, th : 2 * th, :]
        near[p, 2 * nz * th :, :] = sp


def powers(t2, u2, gain, r):
    x = mm(t2[r * RC : (r + 1) * RC, :], u2, 1, 0)
    if gain is not None:
        x = x + jnp.concatenate([gain[r * RC : (r + 1) * RC, :]] * (CB // 128), axis=1)
    return jnp.exp2(x)


def balance(t2, uh_ref, gain, scr, acc, first, finish, carry):
    n = uh_ref.shape[1] // CB
    acc[...] = jnp.zeros_like(acc)

    def block(j):
        return uh_ref[:, pl.ds(pl.multiple_of(j * CB, CB), CB)]

    def half(j, src, dst, b, carry):
        col = jnp.zeros((8, CB), F32)
        if dst is not None:
            uh = block(j)
            u2 = jnp.concatenate([uh, uh], axis=0)
        for r in range(t2.shape[0] // RC):
            rows = slice(r * RC, (r + 1) * RC)
            if dst is not None:
                e = powers(t2, u2, gain, r)
                scr[dst, rows, :] = e
                col = col + jnp.sum(e.reshape(RC // 8, 8, CB), axis=0)
            if src is not None:
                e = scr[src, rows, :]
                total = acc[rows, :]
                for k in range(CB // 128):
                    lanes = slice(k * 128, (k + 1) * 128)
                    total = total + e[:, lanes] * b[:, lanes]
                acc[rows, :] = total
        if src is not None and finish is not None:
            carry = finish(j - 1, b, scr.at[src], block(j - 1), carry)
        if dst is not None and first is not None:
            carry = first(uh, carry)
        return 1.0 / jnp.sum(col, axis=0, keepdims=True), carry

    b, carry = half(0, None, 0, None, carry)

    def step(i, state):
        b, carry = half(2 * i + 1, 0, 1, *state)
        return half(2 * i + 2, 1, 0, b, carry)

    b, carry = lax.fori_loop(0, n // 2 - 1, step, (b, carry))
    b, carry = half(n - 1, 0, 1, b, carry)
    return half(n, 1, None, b, carry)[1]


def pass1_kernel(nz, nx, peers, th, sh, near, other, uh_ref, t2, s_half, mixed, e1_out, pay, scr, acc, es_scr, s_acc):
    rows_t = nz * th
    core = lax.axis_index("c")
    for g in range(2 * nx):
        both = jnp.where(core == g % 2, near[g // 2], other[g // 2])
        t = both[:rows_t].astype(BF16).astype(F32) * TEACH_GAIN
        hi = t.astype(BF16)
        t2[g * rows_t : (g + 1) * rows_t, 0:BOT] = hi
        t2[g * rows_t : (g + 1) * rows_t, BOT : 2 * BOT] = (t - hi.astype(F32)).astype(BF16)
        mixed[g * rows_t : (g + 1) * rows_t, :] = both[rows_t : 2 * rows_t]
        s_half[g * sh : (g + 1) * sh, :] = both[2 * rows_t :].astype(BF16)
    s_acc[...] = jnp.zeros_like(s_acc)
    n_t, n_s = t2.shape[0] // 128, s_half.shape[0] // 128
    own = pl.multiple_of(lax.axis_index("x") * 2 * sh, 2 * sh)

    def first(uh, e1):
        for r in range(s_half.shape[0] // 128):
            rows = slice(r * 128, (r + 1) * 128)
            es = jnp.exp2(mm(s_half[rows, :], uh, 1, 0) * STUD_GAIN)
            es_scr[rows, :] = es
            s_acc[rows, :] += sum(es[:, k * 128 : (k + 1) * 128] for k in range(CB // 128))
        return e1 + mm(es_scr[pl.ds(own, 2 * sh), :].astype(BF16), uh, 1, 1)

    e1 = balance(t2, uh_ref, None, scr, acc, first, None, jnp.zeros((2 * sh, BOT), F32))
    sums = lane_sums(acc, n_t)
    totals = jnp.concatenate([lane_sums(s_acc, n_s), jnp.zeros((8 - n_s, 128), F32)], axis=0)
    e1_out[...] = e1
    for p in range(peers):
        pay[p, 0:n_t, :] = sums
        pay[p, n_t : n_t + 8, :] = totals


def total_of(ref, start, rows):
    total = ref[0, start : start + rows, :]
    for p in range(1, ref.shape[0]):
        total = total + ref[p, start : start + rows, :]
    return total


def student_kernel(nz, nx, own, n_t, n_s, ex1, s_half, uh_ref, log_a1, out, token, scale, prob_scr):
    token[...] = jnp.zeros_like(token)
    scale[...] = spread(GRAD_GAIN / total_of(ex1, n_t, 8)[:n_s])
    shape = (nz * own, BOT)
    row = lax.broadcasted_iota(jnp.int32, shape, 0)
    lane = lax.broadcasted_iota(jnp.int32, shape, 1)
    base = lax.axis_index("x") * own
    pick = jnp.zeros(shape, jnp.bool_)
    for i in range(own):
        for z in range(nz):
            pick = pick | ((row == i * nz + z) & (lane == z * nx * own + base + i))
    picked = mm(jnp.where(pick, 1.0, 0.0).astype(BF16), s_half[...], 1, 1).astype(BF16)
    n_c = uh_ref.shape[1] // 128
    per = (own + 1) * n_c

    def step(j, carry):
        uh = uh_ref[:, pl.ds(pl.multiple_of(j * CB, CB), CB)]
        dots = jnp.zeros((8, CB), F32)
        for r in range(s_half.shape[0] // 128):
            rows = slice(r * 128, (r + 1) * 128)
            logits = mm(s_half[rows, :], uh, 1, 0)
            prob = jnp.exp2(logits * STUD_GAIN) * jnp.concatenate([scale[rows, :]] * (CB // 128), axis=1)
            dots = dots + jnp.sum((prob * logits).reshape(16, 8, CB), axis=0)
            prob_scr[rows, :] = prob.astype(BF16)
        d = mm(picked, prob_scr[...], 1, 0)
        dot_row = jnp.broadcast_to(jnp.sum(dots, axis=0, keepdims=True), (nz, CB))
        for k in range(CB // 128):
            lanes = slice(k * 128, (k + 1) * 128)
            at = j * (CB // 128) + k
            for i in range(own):
                out[pl.ds(i * n_c + at, nz, stride=per), :] = d[i * nz : (i + 1) * nz, lanes]
            out[pl.ds(own * n_c + at, nz, stride=per), :] = dot_row[:, lanes]
        return carry

    lax.fori_loop(0, uh_ref.shape[1] // CB, step, 0)


def pass2_kernel(peers, n_t, ex1, e1, t2, uh_ref, pay, log_a, scr, acc, gain):
    la = jnp.log(total_of(ex1, 0, n_t)) * -LOG2E
    log_a[...] = la
    gain[...] = spread(la)
    part = e1.shape[0] // peers
    fill = jnp.zeros((16 - part, BOT), F32)
    balance(t2, uh_ref, gain, scr, acc, None, None, 0)
    sums = lane_sums(acc, n_t)
    for p in range(peers):
        pay[p, 0:n_t, :] = sums
        pay[p, n_t : n_t + 16, :] = jnp.concatenate([e1[p * part : (p + 1) * part, :], fill], axis=0)


def own_rows(nz, th, g):
    z, x = lax.axis_index("z"), lax.axis_index("x")
    return [pl.multiple_of(((2 * x + c) * nz + z) * th, th) for c in range(g)]


def pass3_kernel(nz, th, n_t, ex2, log_a1, t2, uh_ref, token, pay, log_a2, b_out, scr, acc, gain):
    la = log_a1[...] - jnp.log(total_of(ex2, 0, n_t)) * LOG2E
    log_a2[...] = la
    gain[...] = spread(la)
    starts = own_rows(nz, th, 2)

    def finish(j, b, block, uh, t_sum):
        b_out[:, pl.ds(pl.multiple_of(j * CB, CB), CB)] = b
        mine = jnp.concatenate([block[pl.ds(s, th), :] for s in starts], axis=0) * b
        return t_sum + mm(mine.astype(BF16), uh, 1, 1)

    t_sum = balance(t2, uh_ref, gain, scr, acc, None, finish, jnp.zeros((2 * th, BOT), F32))
    pay[0:n_t, :] = lane_sums(acc, n_t)
    pay[n_t : n_t + 2 * th, :] = t_sum
    pay[n_t + 2 * th :, :] = total_of(ex2, n_t, 16)


def final_kernel(
    nz, nx, own, th, sh, n_t, n_s,
    ex3, log_a2, b_ref, t2, uh_ref, mixed, ex1, student, image, kind,
    d2_out, gs, gain, ma, s_scr, scr,
):
    x, z = lax.axis_index("x"), lax.axis_index("z")
    peers = ex3.shape[0]
    ratio = 1.0 / total_of(ex3, 0, n_t)
    gain[...] = spread(ratio)
    s_scr[...] = spread(1.0 / total_of(ex1, n_t, 8)[:n_s])
    own_ratio = jnp.concatenate([gain[pl.ds(s, th), :] for s in own_rows(nz, th, 2)], axis=0)
    t_sum = total_of(ex3, n_t, 2 * th) * own_ratio
    part = 2 * sh // peers
    e1 = jnp.concatenate([ex3[p, n_t + 2 * th : n_t + 2 * th + part, :] for p in range(peers)], axis=0)
    e1 = e1 * s_scr[pl.ds(pl.multiple_of(x * 2 * sh, 2 * sh), 2 * sh), :]
    weights = selector(image[...], kind[...], 2 * th)
    dz = GRAD_GAIN * (e1 - mm(weights, t_sum, 0, 0, HI))
    s_unit, s_norm = row_unit(student[...].astype(F32))
    gs[...] = (dz - s_unit * jnp.sum(s_unit * dz, axis=1, keepdims=True)) / s_norm
    gain[...] = spread(jnp.exp2(log_a2[...]) * ratio)
    for i in range(n_t):
        rows = slice(i * 128, (i + 1) * 128)
        ma[:, rows] = (mixed[rows, :] * gain[rows, :]).T.astype(BF16)
    start = (z * nx + x) * own
    n = uh_ref.shape[1] // CB

    def fill(j, dst):
        uh = uh_ref[:, pl.ds(pl.multiple_of(j * CB, CB), CB)]
        u2 = jnp.concatenate([uh, uh], axis=0)
        for r in range(t2.shape[0] // RC):
            scr[dst, r * RC : (r + 1) * RC, :] = powers(t2, u2, None, r).astype(BF16)

    def use(j, src):
        cols = pl.ds(pl.multiple_of(j * CB, CB), CB)
        d2 = mm(ma[...], scr[src], 1, 0) * (b_ref[:, cols] * GRAD_GAIN)
        dots2 = jnp.sum(uh_ref[:, cols].astype(F32) * d2, axis=0, keepdims=True)
        row = lax.broadcasted_iota(jnp.int32, d2.shape, 0)

        outs = [jnp.sum(jnp.where(row == start + i, d2, 0.0), axis=0, keepdims=True) for i in range(own)]
        d2_out[:, cols] = jnp.concatenate(outs + [dots2], axis=0)

    fill(0, 0)

    def step(i, carry):
        fill(2 * i + 1, 1)
        use(2 * i, 0)
        fill(2 * i + 2, 0)
        use(2 * i + 1, 1)
        return carry

    lax.fori_loop(0, n // 2 - 1, step, 0)
    fill(n - 1, 1)
    use(n - 2, 0)
    use(n - 1, 1)


def join_kernel(own, d1, d2, norm, mine, gp, d_scr):
    total = d1[0]
    for k in range(1, d1.shape[0]):
        total = total + d1[k]
    d_scr[...] = total
    n_c = norm.shape[1] // 128
    for k in range(n_c):
        cols = slice(k * 128, (k + 1) * 128)
        dots = d_scr[own * n_c + k : own * n_c + k + 1, :] - d2[own : own + 1, cols]
        early = jnp.concatenate([d_scr[i * n_c + k : i * n_c + k + 1, :] for i in range(own)], axis=0)
        gp[:, cols] = (early - d2[0:own, cols] - mine[:, cols] * dots) / norm[:, cols]


def sds(shape, dtype=F32):
    return jax.ShapeDtypeStruct(shape, dtype)


def swap(x, axes):
    return lax.all_to_all(x, axes, 0, 0, tiled=True)


def per_device(sizes, student_feat, teacher_feat, prototypes, crop_image, crop_kind):
    nz, nx, ny, nc = sizes
    peers = ny * nc
    crops, teach = student_feat.shape[0], teacher_feat.shape[0]
    th, sh = teach // 2, crops // 2
    cols = prototypes.shape[1]
    own = BOT // (nz * nx)
    teachers, gathered = teach * nz * nx, crops * nx
    n_t, n_s = teachers // 128, gathered // 128
    image, kind = crop_image.reshape(1, crops), crop_kind.reshape(1, crops)
    fl = 2 * teachers * cols * 256

    zp = call(
        functools.partial(prep_kernel, nz),
        sds((nz, 2 * th, BOT)),
        student_feat,
        teacher_feat,
        image,
        kind,
        limit=58 * 1024 * 1024,
    )
    half, norm, mine = call(
        functools.partial(unit_kernel, own, nx),
        (sds((BOT, cols), BF16), sds((1, cols)), sds((own, cols))),
        prototypes,
        flops=fl // 2,
    )
    got = swap(zp, "z")
    near = call(
        functools.partial(pack_kernel, nz, nx),
        sds((nx, 2 * nz * th + sh, BOT)),
        got,
        student_feat,
    )
    near = swap(near, "x")
    other = lax.ppermute(near, "c", [(0, 1), (1, 0)])

    big = [pltpu.VMEM((2, teachers, CB), F32), pltpu.VMEM((teachers, 128), F32)]
    t2, s_half, mixed, e1, pay1 = call(
        functools.partial(pass1_kernel, nz, nx, peers, th, sh),
        (sds((teachers, 256), BF16), sds((gathered, BOT), BF16), sds((teachers, BOT)), sds((crops, BOT)), sds((peers, n_t + 8, 128))),
        near,
        other,
        half,
        scratch=big + [pltpu.VMEM((gathered, CB), F32), pltpu.VMEM((gathered, 128), F32)],
        flops=fl,
    )
    ex1 = swap(pay1, ("y", "c"))
    pay2, log_a1 = call(
        functools.partial(pass2_kernel, peers, n_t),
        (sds((peers, n_t + 16, 128)), sds((n_t, 128))),
        ex1,
        e1,
        t2,
        half,
        scratch=big + [pltpu.VMEM((teachers, 128), F32)],
        flops=fl // 4,
    )
    ex2 = swap(pay2, ("y", "c"))
    d1, token = call(
        functools.partial(student_kernel, nz, nx, own, n_t, n_s),
        (sds((nz * (own + 1) * cols // 128, 128)), sds((8, 128))),
        ex1,
        s_half,
        half,
        log_a1,
        scratch=[pltpu.VMEM((gathered, 128), F32), pltpu.VMEM((gathered, CB), BF16)],
        flops=fl // 2,
    )
    d1 = swap(d1.reshape(nz, (own + 1) * cols // 128, 128), "z")
    pay3, log_a2, b3 = call(
        functools.partial(pass3_kernel, nz, th, n_t),
        (sds((n_t + teach + 16, 128)), sds((n_t, 128)), sds((1, cols))),
        ex2,
        log_a1,
        t2,
        half,
        token,
        scratch=big + [pltpu.VMEM((teachers, 128), F32)],
        flops=fl // 4,
    )
    ex3 = lax.all_gather(pay3, ("y", "c"))
    d2, grad_student = call(
        functools.partial(final_kernel, nz, nx, own, th, sh, n_t, n_s),
        (sds((own + 1, cols)), sds((crops, BOT))),
        ex3, log_a2, b3, t2, half, mixed, ex1, student_feat, image, kind,
        scratch=[
            pltpu.VMEM((teachers, 128), F32),
            pltpu.VMEM((BOT, teachers), BF16),
            pltpu.VMEM((gathered, 128), F32),
            pltpu.VMEM((2, teachers, CB), BF16),
        ],
        flops=fl * 2,
    )
    grad_proto = call(
        functools.partial(join_kernel, own),
        sds((own, cols)),
        d1,
        d2,
        norm,
        mine,
        scratch=[pltpu.VMEM(((own + 1) * cols // 128, 128), F32)],
    )
    return grad_proto, grad_student


def build(devices):
    grid = Mesh(devices, ("z", "x", "y", "c"))
    batch, proto = ("z", "x"), ("y", "c")
    return jax.shard_map(
        functools.partial(per_device, devices.shape),
        mesh=grid,
        in_specs=(P(batch, None), P(batch, None), P(None, proto), P(batch), P(batch)),
        out_specs=(P(batch, proto), P(batch, None)),
        check_vma=False,
    )


def solution(mesh):
    return build(mesh.devices.reshape(16, 4, 8, 2))
```

```python
import functools

import jax
import jax.numpy as jnp
from jax import lax
from jax.experimental import pallas as pl
from jax.experimental.pallas import tpu as pltpu
from jax.sharding import Mesh
from jax.sharding import PartitionSpec as P

LOSS_SCALE = 16
EPS = 1e-06
LOG2E = 1.4426950408889634
TEACH_GAIN = 25.0 * LOG2E
STUD_GAIN = 10.0 * LOG2E
GRAD_GAIN = 160.0
BOT = 128
CB = 512
RC = 256
IMGS = 16
F32 = jnp.float32
BF16 = jnp.bfloat16
HI = lax.Precision.HIGHEST
VMEM_LIMIT = 16 * 1024 * 1024
INTERPRET = False


def mm(a, b, ca, cb, precision=None):
    return lax.dot_general(a, b, (((ca,), (cb,)), ((), ())), precision=precision, preferred_element_type=F32)


def call(kernel, out_shape, *args, scratch=(), flops=0, limit=VMEM_LIMIT):
    specs = pl.BlockSpec(memory_space=pltpu.VMEM)
    return pl.pallas_call(
        kernel,
        out_shape=out_shape,
        in_specs=[specs] * len(args),
        out_specs=jax.tree.map(lambda _: specs, out_shape),
        scratch_shapes=list(scratch),
        compiler_params=pltpu.CompilerParams(vmem_limit_bytes=limit),
        cost_estimate=pl.CostEstimate(flops=flops, bytes_accessed=0, transcendentals=0),
        interpret=INTERPRET,
    )(*args)


def row_unit(x):
    norm = jnp.sqrt(jnp.sum(x * x, axis=-1, keepdims=True) + EPS)
    return x / norm, norm


def selector(image, kind, teach_rows):
    shape = (teach_rows, image.shape[1])
    teach = lax.broadcasted_iota(jnp.int32, shape, 0)
    local = jnp.bitwise_and(jnp.broadcast_to(image, shape), IMGS - 1)
    kinds = jnp.broadcast_to(kind, shape)
    weight = jnp.where(kinds == 0, 0.5, jnp.where(jnp.bitwise_and(teach, 1) == 2 - kinds, 1.0, 0.0))
    return jnp.where(local == jnp.right_shift(teach, 1), weight, 0.0)


def spread(rows):
    parts = [jnp.broadcast_to(rows[i : i + 1, :], (128, 128)).T for i in range(rows.shape[0])]
    return jnp.concatenate(parts, axis=0)


def lane_sums(ref, n):
    parts = [jnp.sum(ref[i * 128 : (i + 1) * 128, :].T, axis=0, keepdims=True) for i in range(n)]
    return jnp.concatenate(parts, axis=0)


def prep_kernel(nz, student, teacher, image, kind, zp):
    s_unit = row_unit(student[...].astype(F32))[0]
    t_unit = row_unit(teacher[...].astype(F32))[0]
    weights = selector(image[...], kind[...], teacher.shape[0])
    mixed = mm(weights.astype(BF16), s_unit.astype(BF16), 1, 0)
    th = teacher.shape[0] // 2
    first = lax.axis_index("c") == 0
    t = jnp.where(first, t_unit[:th], t_unit[th:])
    m = jnp.where(first, mixed[:th], mixed[th:])
    for p in range(nz):
        zp[p, 0:th, :] = t
        zp[p, th : 2 * th, :] = m


def unit_kernel(own, nx, proto, half, norm, mine):
    start = (lax.axis_index("z") * nx + lax.axis_index("x")) * own

    def step(j, carry):
        cols = pl.ds(pl.multiple_of(j * CB, CB), CB)
        v = proto[:, cols]
        n = jnp.sqrt(jnp.sum(v * v, axis=0, keepdims=True) + EPS)
        unit = v / n
        half[:, cols] = unit.astype(BF16)
        norm[:, cols] = n
        row = lax.broadcasted_iota(jnp.int32, unit.shape, 0)
        mine[:, cols] = jnp.concatenate(
            [jnp.sum(jnp.where(row == start + i, unit, 0.0), axis=0, keepdims=True) for i in range(own)], axis=0
        )
        return carry

    lax.fori_loop(0, proto.shape[1] // CB, step, 0)


def pack_kernel(nz, nx, got, student, near):
    th, sh = got.shape[1] // 2, student.shape[0] // 2
    s_unit = row_unit(student[...].astype(F32))[0]
    sp = jnp.where(lax.axis_index("c") == 0, s_unit[:sh], s_unit[sh:])
    for p in range(nx):
        for z in range(nz):
            near[p, z * th : (z + 1) * th, :] = got[z, 0:th, :]
            near[p, (nz + z) * th : (nz + z + 1) * th, :] = got[z, th : 2 * th, :]
        near[p, 2 * nz * th :, :] = sp


def powers(t2, u2, gain, r):
    x = mm(t2[r * RC : (r + 1) * RC, :], u2, 1, 0)
    if gain is not None:
        x = x + jnp.concatenate([gain[r * RC : (r + 1) * RC, :]] * (CB // 128), axis=1)
    return jnp.exp2(x)


def balance(t2, uh_ref, gain, scr, acc, first, finish, carry):
    n = uh_ref.shape[1] // CB
    acc[...] = jnp.zeros_like(acc)

    def block(j):
        return uh_ref[:, pl.ds(pl.multiple_of(j * CB, CB), CB)]

    def half(j, src, dst, b, carry):
        col = jnp.zeros((8, CB), F32)
        if dst is not None:
            uh = block(j)
            u2 = jnp.concatenate([uh, uh], axis=0)
        for r in range(t2.shape[0] // RC):
            rows = slice(r * RC, (r + 1) * RC)
            if dst is not None:
                e = powers(t2, u2, gain, r)
                scr[dst, rows, :] = e
                col = col + jnp.sum(e.reshape(RC // 8, 8, CB), axis=0)
            if src is not None:
                e = scr[src, rows, :]
                total = acc[rows, :]
                for k in range(CB // 128):
                    lanes = slice(k * 128, (k + 1) * 128)
                    total = total + e[:, lanes] * b[:, lanes]
                acc[rows, :] = total
        if src is not None and finish is not None:
            carry = finish(j - 1, b, scr.at[src], block(j - 1), carry)
        if dst is not None and first is not None:
            carry = first(uh, carry)
        return 1.0 / jnp.sum(col, axis=0, keepdims=True), carry

    b, carry = half(0, None, 0, None, carry)

    def step(i, state):
        b, carry = half(2 * i + 1, 0, 1, *state)
        return half(2 * i + 2, 1, 0, b, carry)

    b, carry = lax.fori_loop(0, n // 2 - 1, step, (b, carry))
    b, carry = half(n - 1, 0, 1, b, carry)
    return half(n, 1, None, b, carry)[1]


def pass1_kernel(nz, nx, peers, th, sh, near, other, uh_ref, t2, s_half, mixed, e1_out, pay, scr, acc, es_scr, s_acc):
    rows_t = nz * th
    core = lax.axis_index("c")
    for g in range(2 * nx):
        both = jnp.where(core == g % 2, near[g // 2], other[g // 2])
        t = both[:rows_t].astype(BF16).astype(F32) * TEACH_GAIN
        hi = t.astype(BF16)
        t2[g * rows_t : (g + 1) * rows_t, 0:BOT] = hi
        t2[g * rows_t : (g + 1) * rows_t, BOT : 2 * BOT] = (t - hi.astype(F32)).astype(BF16)
        mixed[g * rows_t : (g + 1) * rows_t, :] = both[rows_t : 2 * rows_t]
        s_half[g * sh : (g + 1) * sh, :] = both[2 * rows_t :].astype(BF16)
    s_acc[...] = jnp.zeros_like(s_acc)
    n_t, n_s = t2.shape[0] // 128, s_half.shape[0] // 128
    own = pl.multiple_of(lax.axis_index("x") * 2 * sh, 2 * sh)

    def first(uh, e1):
        for r in range(s_half.shape[0] // 128):
            rows = slice(r * 128, (r + 1) * 128)
            es = jnp.exp2(mm(s_half[rows, :], uh, 1, 0) * STUD_GAIN)
            es_scr[rows, :] = es
            s_acc[rows, :] += sum(es[:, k * 128 : (k + 1) * 128] for k in range(CB // 128))
        return e1 + mm(es_scr[pl.ds(own, 2 * sh), :].astype(BF16), uh, 1, 1)

    e1 = balance(t2, uh_ref, None, scr, acc, first, None, jnp.zeros((2 * sh, BOT), F32))
    sums = lane_sums(acc, n_t)
    totals = jnp.concatenate([lane_sums(s_acc, n_s), jnp.zeros((8 - n_s, 128), F32)], axis=0)
    e1_out[...] = e1
    for p in range(peers):
        pay[p, 0:n_t, :] = sums
        pay[p, n_t : n_t + 8, :] = totals


def total_of(ref, start, rows):
    total = ref[0, start : start + rows, :]
    for p in range(1, ref.shape[0]):
        total = total + ref[p, start : start + rows, :]
    return total


def student_kernel(nz, nx, own, n_t, n_s, ex1, s_half, uh_ref, log_a1, out, token, scale, prob_scr):
    token[...] = jnp.zeros_like(token)
    scale[...] = spread(GRAD_GAIN / total_of(ex1, n_t, 8)[:n_s])
    shape = (nz * own, BOT)
    row = lax.broadcasted_iota(jnp.int32, shape, 0)
    lane = lax.broadcasted_iota(jnp.int32, shape, 1)
    base = lax.axis_index("x") * own
    pick = jnp.zeros(shape, jnp.bool_)
    for i in range(own):
        for z in range(nz):
            pick = pick | ((row == i * nz + z) & (lane == z * nx * own + base + i))
    picked = mm(jnp.where(pick, 1.0, 0.0).astype(BF16), s_half[...], 1, 1).astype(BF16)
    n_c = uh_ref.shape[1] // 128
    per = (own + 1) * n_c

    def step(j, carry):
        uh = uh_ref[:, pl.ds(pl.multiple_of(j * CB, CB), CB)]
        dots = jnp.zeros((8, CB), F32)
        for r in range(s_half.shape[0] // 128):
            rows = slice(r * 128, (r + 1) * 128)
            logits = mm(s_half[rows, :], uh, 1, 0)
            prob = jnp.exp2(logits * STUD_GAIN) * jnp.concatenate([scale[rows, :]] * (CB // 128), axis=1)
            dots = dots + jnp.sum((prob * logits).reshape(16, 8, CB), axis=0)
            prob_scr[rows, :] = prob.astype(BF16)
        d = mm(picked, prob_scr[...], 1, 0)
        dot_row = jnp.broadcast_to(jnp.sum(dots, axis=0, keepdims=True), (nz, CB))
        for k in range(CB // 128):
            lanes = slice(k * 128, (k + 1) * 128)
            at = j * (CB // 128) + k
            for i in range(own):
                out[pl.ds(i * n_c + at, nz, stride=per), :] = d[i * nz : (i + 1) * nz, lanes]
            out[pl.ds(own * n_c + at, nz, stride=per), :] = dot_row[:, lanes]
        return carry

    lax.fori_loop(0, uh_ref.shape[1] // CB, step, 0)


def pass2_kernel(peers, n_t, ex1, e1, t2, uh_ref, pay, log_a, scr, acc, gain):
    la = jnp.log(total_of(ex1, 0, n_t)) * -LOG2E
    log_a[...] = la
    gain[...] = spread(la)
    part = e1.shape[0] // peers
    fill = jnp.zeros((16 - part, BOT), F32)
    balance(t2, uh_ref, gain, scr, acc, None, None, 0)
    sums = lane_sums(acc, n_t)
    for p in range(peers):
        pay[p, 0:n_t, :] = sums
        pay[p, n_t : n_t + 16, :] = jnp.concatenate([e1[p * part : (p + 1) * part, :], fill], axis=0)


def own_rows(nz, th, g):
    z, x = lax.axis_index("z"), lax.axis_index("x")
    return [pl.multiple_of(((2 * x + c) * nz + z) * th, th) for c in range(g)]


def pass3_kernel(nz, th, n_t, ex2, log_a1, t2, uh_ref, token, pay, log_a2, b_out, scr, acc, gain, own_scr):
    la = log_a1[...] - jnp.log(total_of(ex2, 0, n_t)) * LOG2E
    log_a2[...] = la
    gain[...] = spread(la)
    starts = own_rows(nz, th, 2)

    def finish(j, b, block, uh, t_sum):
        b_out[:, pl.ds(pl.multiple_of(j * CB, CB), CB)] = b
        mine = jnp.concatenate([block[pl.ds(s, th), :] for s in starts], axis=0) * b
        own_scr[:, pl.ds(pl.multiple_of(j * CB, CB), CB)] = mine.astype(BF16)
        return t_sum

    balance(t2, uh_ref, gain, scr, acc, None, finish, 0)
    t_sum = mm(own_scr[...], uh_ref[...], 1, 1)
    pay[0:n_t, :] = lane_sums(acc, n_t)
    pay[n_t : n_t + 2 * th, :] = t_sum
    pay[n_t + 2 * th :, :] = total_of(ex2, n_t, 16)


def final_kernel(
    nz, nx, own, th, sh, n_t, n_s,
    ex3, log_a2, b_ref, t2, uh_ref, mixed, ex1, student, image, kind,
    d2_out, gs, gain, ma, s_scr, scr,
):
    x, z = lax.axis_index("x"), lax.axis_index("z")
    peers = ex3.shape[0]
    ratio = 1.0 / total_of(ex3, 0, n_t)
    gain[...] = spread(ratio)
    s_scr[...] = spread(1.0 / total_of(ex1, n_t, 8)[:n_s])
    own_ratio = jnp.concatenate([gain[pl.ds(s, th), :] for s in own_rows(nz, th, 2)], axis=0)
    t_sum = total_of(ex3, n_t, 2 * th) * own_ratio
    part = 2 * sh // peers
    e1 = jnp.concatenate([ex3[p, n_t + 2 * th : n_t + 2 * th + part, :] for p in range(peers)], axis=0)
    e1 = e1 * s_scr[pl.ds(pl.multiple_of(x * 2 * sh, 2 * sh), 2 * sh), :]
    weights = selector(image[...], kind[...], 2 * th)
    dz = GRAD_GAIN * (e1 - mm(weights, t_sum, 0, 0, HI))
    s_unit, s_norm = row_unit(student[...].astype(F32))
    gs[...] = (dz - s_unit * jnp.sum(s_unit * dz, axis=1, keepdims=True)) / s_norm
    gain[...] = spread(jnp.exp2(log_a2[...]) * ratio)
    for i in range(n_t):
        rows = slice(i * 128, (i + 1) * 128)
        ma[:, rows] = (mixed[rows, :] * gain[rows, :]).T.astype(BF16)
    start = (z * nx + x) * own
    n = uh_ref.shape[1] // CB

    def fill(j, dst):
        uh = uh_ref[:, pl.ds(pl.multiple_of(j * CB, CB), CB)]
        u2 = jnp.concatenate([uh, uh], axis=0)
        for r in range(t2.shape[0] // RC):
            scr[dst, r * RC : (r + 1) * RC, :] = powers(t2, u2, None, r).astype(BF16)

    def use(j, src):
        cols = pl.ds(pl.multiple_of(j * CB, CB), CB)
        d2 = mm(ma[...], scr[src], 1, 0) * (b_ref[:, cols] * GRAD_GAIN)
        dots2 = jnp.sum(uh_ref[:, cols].astype(F32) * d2, axis=0, keepdims=True)
        row = lax.broadcasted_iota(jnp.int32, d2.shape, 0)

        outs = [jnp.sum(jnp.where(row == start + i, d2, 0.0), axis=0, keepdims=True) for i in range(own)]
        d2_out[:, cols] = jnp.concatenate(outs + [dots2], axis=0)

    fill(0, 0)

    def step(i, carry):
        fill(2 * i + 1, 1)
        use(2 * i, 0)
        fill(2 * i + 2, 0)
        use(2 * i + 1, 1)
        return carry

    lax.fori_loop(0, n // 2 - 1, step, 0)
    fill(n - 1, 1)
    use(n - 2, 0)
    use(n - 1, 1)


def join_kernel(own, d1, d2, norm, mine, gp, d_scr):
    total = d1[0]
    for k in range(1, d1.shape[0]):
        total = total + d1[k]
    d_scr[...] = total
    n_c = norm.shape[1] // 128
    for k in range(n_c):
        cols = slice(k * 128, (k + 1) * 128)
        dots = d_scr[own * n_c + k : own * n_c + k + 1, :] - d2[own : own + 1, cols]
        early = jnp.concatenate([d_scr[i * n_c + k : i * n_c + k + 1, :] for i in range(own)], axis=0)
        gp[:, cols] = (early - d2[0:own, cols] - mine[:, cols] * dots) / norm[:, cols]


def sds(shape, dtype=F32):
    return jax.ShapeDtypeStruct(shape, dtype)


def swap(x, axes):
    return lax.all_to_all(x, axes, 0, 0, tiled=True)


def per_device(sizes, student_feat, teacher_feat, prototypes, crop_image, crop_kind):
    nz, nx, ny, nc = sizes
    peers = ny * nc
    crops, teach = student_feat.shape[0], teacher_feat.shape[0]
    th, sh = teach // 2, crops // 2
    cols = prototypes.shape[1]
    own = BOT // (nz * nx)
    teachers, gathered = teach * nz * nx, crops * nx
    n_t, n_s = teachers // 128, gathered // 128
    image, kind = crop_image.reshape(1, crops), crop_kind.reshape(1, crops)
    fl = 2 * teachers * cols * 256

    zp = call(
        functools.partial(prep_kernel, nz),
        sds((nz, 2 * th, BOT)),
        student_feat,
        teacher_feat,
        image,
        kind,
        limit=58 * 1024 * 1024,
    )
    half, norm, mine = call(
        functools.partial(unit_kernel, own, nx),
        (sds((BOT, cols), BF16), sds((1, cols)), sds((own, cols))),
        prototypes,
        flops=fl // 2,
    )
    got = swap(zp, "z")
    near = call(
        functools.partial(pack_kernel, nz, nx),
        sds((nx, 2 * nz * th + sh, BOT)),
        got,
        student_feat,
    )
    near = swap(near, "x")
    other = lax.ppermute(near, "c", [(0, 1), (1, 0)])

    big = [pltpu.VMEM((2, teachers, CB), F32), pltpu.VMEM((teachers, 128), F32)]
    t2, s_half, mixed, e1, pay1 = call(
        functools.partial(pass1_kernel, nz, nx, peers, th, sh),
        (sds((teachers, 256), BF16), sds((gathered, BOT), BF16), sds((teachers, BOT)), sds((crops, BOT)), sds((peers, n_t + 8, 128))),
        near,
        other,
        half,
        scratch=big + [pltpu.VMEM((gathered, CB), F32), pltpu.VMEM((gathered, 128), F32)],
        flops=fl,
    )
    ex1 = swap(pay1, ("y", "c"))
    pay2, log_a1 = call(
        functools.partial(pass2_kernel, peers, n_t),
        (sds((peers, n_t + 16, 128)), sds((n_t, 128))),
        ex1,
        e1,
        t2,
        half,
        scratch=big + [pltpu.VMEM((teachers, 128), F32)],
        flops=fl // 4,
    )
    ex2 = swap(pay2, ("y", "c"))
    d1, token = call(
        functools.partial(student_kernel, nz, nx, own, n_t, n_s),
        (sds((nz * (own + 1) * cols // 128, 128)), sds((8, 128))),
        ex1,
        s_half,
        half,
        log_a1,
        scratch=[pltpu.VMEM((gathered, 128), F32), pltpu.VMEM((gathered, CB), BF16)],
        flops=fl // 2,
    )
    d1 = swap(d1.reshape(nz, (own + 1) * cols // 128, 128), "z")
    pay3, log_a2, b3 = call(
        functools.partial(pass3_kernel, nz, th, n_t),
        (sds((n_t + teach + 16, 128)), sds((n_t, 128)), sds((1, cols))),
        ex2,
        log_a1,
        t2,
        half,
        token,
        scratch=big + [pltpu.VMEM((teachers, 128), F32), pltpu.VMEM((teach, cols), BF16)],
        flops=fl // 4,
    )
    ex3 = lax.all_gather(pay3, ("y", "c"))
    d2, grad_student = call(
        functools.partial(final_kernel, nz, nx, own, th, sh, n_t, n_s),
        (sds((own + 1, cols)), sds((crops, BOT))),
        ex3, log_a2, b3, t2, half, mixed, ex1, student_feat, image, kind,
        scratch=[
            pltpu.VMEM((teachers, 128), F32),
            pltpu.VMEM((BOT, teachers), BF16),
            pltpu.VMEM((gathered, 128), F32),
            pltpu.VMEM((2, teachers, CB), BF16),
        ],
        flops=fl * 2,
    )
    grad_proto = call(
        functools.partial(join_kernel, own),
        sds((own, cols)),
        d1,
        d2,
        norm,
        mine,
        scratch=[pltpu.VMEM(((own + 1) * cols // 128, 128), F32)],
    )
    return grad_proto, grad_student


def build(devices):
    grid = Mesh(devices, ("z", "x", "y", "c"))
    batch, proto = ("z", "x"), ("y", "c")
    return jax.shard_map(
        functools.partial(per_device, devices.shape),
        mesh=grid,
        in_specs=(P(batch, None), P(batch, None), P(None, proto), P(batch), P(batch)),
        out_specs=(P(batch, proto), P(batch, None)),
        check_vma=False,
    )


def solution(mesh):
    return build(mesh.devices.reshape(16, 4, 8, 2))
```
